128 devices in a mesh: req: 16 (over y, x), tp: 8 (over z, core).
Axes of the slice: x: 4, y: 4, z: 4, core: 2. Of those that a mesh axis runs over, the one named last changes fastest.
Arguments:
- queries: bfloat16 [256, 8192], P('req', 'tp'), may hold values from -192 to 192
- fresh_key_value: bfloat16 [256, 8, 256], P('req', 'tp'), may hold values from -8 to 8
- key_value_pool: bfloat16 [512, 256, 8, 256], P('req', None, 'tp'), may hold values from -8 to 8
- request_page_table: int32 [256, 4], P('req'), may hold values from 0 to 63, as said below
- cached_length: int32 [256], P('req'), may hold values from 1 to 1024, as said below
- move_holder_shard: int32 [512, 1], P('req'), may hold values from 0 to 15; in each aligned block of 32 rows (0 to 31, 32 to 63, ...) at most 4 rows name the same one
- move_page_index: int32 [512], P('req'), may hold values from 0 to 31
- request_adapter: int32 [256], P('req'), may hold values from 0 to 63
- adapter_storage_slot: int32 [64], replicated, may hold values from 0 to 63, each once
- output_projection: bfloat16 [8192, 8192], P('tp'), may hold values from -0.0625 to 0.0625
- adapter_down_panels: bfloat16 [64, 8192, 64], P('req', 'tp'), may hold values from -0.0625 to 0.0625
- adapter_up_panels: bfloat16 [64, 64, 8192], P('req', None, 'tp'), may hold values from -0.75 to 0.75
Outputs:
- layer_out: bfloat16 [256, 8192], P('req', 'tp')
The draws below stay inside these ranges and needn't reach their ends.
Inputs may be any that keep to these rules, and one draw needn't show every extreme that they name: `move_holder_shard`: in each aligned block of 32 moves (those of one shard) no holder appears more than 4 times; some holder appears exactly 4 times in some blocks. `request_page_table`: within each block of 16 requests the 64 entries are all different, so each entry of a shard's extended page list serves exactly one page of one request. `cached_length`: each block of 16 requests holds one request of 1024 tokens.
All inputs are finite; a program needn't handle non-finite values.
Results may differ from the reference program's by a relative error of at most 0.0095.
Values may be sent and summed in bfloat16 or wider, within the bound.
A program may use at most 128 MiB of HBM per device.

```python
import math
import jax
import jax.numpy as jnp
import numpy as np
from jax import lax

MODEL_WIDTH = 8192
QUERY_HEADS = 64
KV_HEADS = 8
HEAD_SIZE = 128
ADAPTER_RANK = 64
PAGE = 256
MAXP = 4
CAP = 4
REQ_DEV = 16
MOVES = 32
POOL = 32
REQS = 256
POOLS = 512
TOTAL_MOVES = 512
ADAPTER_COUNT = 64
N_REQ = 16


def draw_queries(key, part):
    key = jax.random.fold_in(key, 11)
    base = jnp.clip(jax.random.normal(key, (REQS, QUERY_HEADS, HEAD_SIZE), jnp.float32), -4.0, 4.0)
    return base.reshape(REQS, QUERY_HEADS * HEAD_SIZE).astype(jnp.bfloat16)


def draw_request_page_table(key, part):
    key = jax.random.fold_in(key, 23)
    shard_keys = jax.random.split(key, REQS // REQ_DEV)
    orders = jax.vmap(lambda one_key: jax.random.permutation(one_key, REQ_DEV * MAXP))(shard_keys)
    return orders.reshape(REQS, MAXP).astype(jnp.int32)


def draw_cached_length(key, part):
    key = jax.random.fold_in(key, 37)
    first_key, second_key = jax.random.split(key)
    shards = REQS // REQ_DEV
    lengths = jax.random.randint(first_key, (REQS,), 1, MAXP * PAGE + 1)
    chosen = jax.random.randint(second_key, (shards,), 0, REQ_DEV)
    full_rows = (jnp.arange(REQ_DEV)[None, :] == chosen[:, None]).reshape(REQS)
    return jnp.where(full_rows, MAXP * PAGE, lengths).astype(jnp.int32)


def with_ends(entries, stream_key, smallest, top_value):
    longest = entries.shape.index(max(entries.shape))
    spots = []
    for shift in (0, 1):
        where = [jax.random.randint(jax.random.fold_in(stream_key, axis), (), 0, length) for axis, length in enumerate(entries.shape)]
        where[longest] = (where[longest] + shift) % entries.shape[longest]
        spots.append(tuple(where))
    return entries.at[spots[0]].set(smallest).at[spots[1]].set(top_value)


def shard_levels(own_key, extent, cuts, smallest, top_value):
    def one(dim, blocks):
        draws = jax.random.uniform(jax.random.fold_in(jax.random.fold_in(own_key, 6), dim), (blocks,), jnp.float32, smallest / len(cuts), top_value / len(cuts))
        return jnp.repeat(jnp.exp(draws), extent[dim] // blocks).reshape((-1,) + (1,) * (len(extent) - dim - 1))

    level = one(*cuts[0])
    for cut in cuts[1:]:
        level = level * one(*cut)
    return level


def rank_table(number_of, lean):
    portions = [(1 << 20) // math.isqrt(standing ** lean) + 1 for standing in range(1, number_of + 1)]
    deviation = 1 + sum(portions) // (1 << 30)
    return np.cumsum(np.array([max(1, weight // deviation) for weight in portions]))


def ranked_ids(own_key, shape, amount, skew):
    grid = rank_table(amount, skew)
    lot = jax.random.randint(jax.random.fold_in(own_key, 1), shape, 0, int(grid[amount - 1]))
    grade = jnp.searchsorted(jnp.asarray(grid, jnp.int32), lot, side="right")
    return jax.random.permutation(jax.random.fold_in(own_key, 2), amount)[grade].astype(jnp.int32)


def deal_out(own_key, own, number, rows, amount, top, reach, slope):
    order = jax.random.permutation(own_key, amount)
    packed, ordinary = load_shares(amount, rows * top, reach, slope, True), load_shares(amount, rows * top, reach, slope, False)
    places = jnp.arange(amount)

    def named(tallies, offset_by):
        used = int((tallies > 0).sum())
        fixed = max(1, used // 4)
        shifted = fixed + (places - fixed + offset_by * (used - fixed)) % max(1, amount - fixed)
        return jnp.zeros((amount,), jnp.int32).at[order[jnp.where(places < fixed, places, shifted)]].set(jnp.asarray(tallies, jnp.int32))

    tallies = jnp.where(number % 4 == 0, named(packed, number // 4), named(ordinary, number - number // 4 - 1))
    mixed = jax.random.permutation(jax.random.fold_in(own, 3), amount)
    donor, receiver = mixed[0:amount // 2 * 2:2], mixed[1:amount // 2 * 2:2]
    room = jnp.minimum(tallies[donor] - 1, reach - tallies[receiver]) // 2
    room = jnp.where((donor == order[0]) | (receiver == order[0]) | (tallies[receiver] == 0), 0, jnp.maximum(room, 0))
    shifted = jax.random.randint(jax.random.fold_in(own, 4), (amount // 2,), 0, 1 << 20) % (room + 1)
    tallies = tallies.at[donor].add(-shifted).at[receiver].add(shifted)
    members = jnp.searchsorted(jnp.cumsum(tallies), jnp.arange(rows * top), side="right").astype(jnp.int32)
    table = members.reshape(top, rows).T
    table = table[jax.random.permutation(jax.random.fold_in(own, 1), rows)]
    offset_by = jax.random.randint(jax.random.fold_in(own, 2), (rows, 1), 0, top)
    return jnp.take_along_axis(table, (jnp.arange(top)[None, :] + offset_by) % top, axis=1)


def load_shares(number_of, total, most, slope, full):
    loads = [(1 << 20) // math.isqrt(standing ** slope) + 1 for standing in range(1, number_of + 1)]
    largest = most if full else min(most, max(-(-total // number_of), total * loads[0] // sum(loads)))
    least = 1 if total - largest >= number_of - 1 else 0
    holding, surplus = [largest] + [least] * (number_of - 1), total - largest - least * (number_of - 1)
    while surplus > 0:
        free = [i for i in range(1, number_of) if holding[i] < largest] or [i for i in range(1, number_of) if holding[i] < most]
        whole, left = sum([loads[i] for i in free]), surplus
        for i in free:
            more = min(most - holding[i], max(1, left * loads[i] // whole), surplus)
            holding[i] = holding[i] + more
            surplus = surplus - more
    return np.array(holding)


def scatter_about(own_key, shape, scale, most, cuts=(), kind=jnp.bfloat16):
    values = scale * jax.random.normal(own_key, shape, jnp.float32)
    if cuts:
        values = values * shard_levels(own_key, shape, cuts, -0.22, 0.18)
    return jnp.clip(values, -most, most).astype(kind)


def setup_inputs(seed: int = 0) -> dict:
    key_of = jax.random.split(jax.random.key(seed), 13)
    queries = draw_queries(jax.random.fold_in(key_of[12], 71), 0)
    fresh_key_value = scatter_about(key_of[1], (REQS, KV_HEADS, 2 * HEAD_SIZE), 2.0, 8.0, ((0, 16), (1, 8)))
    key_value_pool = scatter_about(key_of[2], (POOLS, PAGE, KV_HEADS, 2 * HEAD_SIZE), 2.0, 8.0, ((0, 16), (2, 8)))
    request_page_table = draw_request_page_table(jax.random.fold_in(key_of[12], 71), 0)
    cached_length = draw_cached_length(jax.random.fold_in(key_of[12], 71), 0)
    move_holder_shard_keys = jax.random.split(jax.random.fold_in(key_of[5], 1), TOTAL_MOVES // MOVES)
    move_holder_shard_turns = jax.random.permutation(jax.random.fold_in(key_of[5], 3), TOTAL_MOVES // MOVES)
    move_holder_shard = jax.vmap(lambda own, number: deal_out(jax.random.fold_in(key_of[5], 2), own, number, MOVES, N_REQ, 1, CAP, 2))(move_holder_shard_keys, move_holder_shard_turns).reshape((TOTAL_MOVES, 1))
    move_page_index = with_ends(jax.random.randint(key_of[6], (TOTAL_MOVES,), 0, POOL), jax.random.fold_in(key_of[6], 1), 0, POOL - 1).astype(jnp.int32)
    request_adapter = with_ends(ranked_ids(key_of[7], (REQS,), ADAPTER_COUNT, 2), jax.random.fold_in(key_of[7], 3), 0, ADAPTER_COUNT - 1).astype(jnp.int32)
    adapter_storage_slot = jax.random.permutation(key_of[8], ADAPTER_COUNT).astype(jnp.int32)
    output_projection = scatter_about(key_of[9], (QUERY_HEADS * HEAD_SIZE, MODEL_WIDTH), (QUERY_HEADS * HEAD_SIZE) ** -0.5, 0.0625, ((0, 8),))
    adapter_down_panels = scatter_about(key_of[10], (ADAPTER_COUNT, QUERY_HEADS * HEAD_SIZE, ADAPTER_RANK), (QUERY_HEADS * HEAD_SIZE) ** -0.5, 0.0625, ((0, 16), (1, 8)))
    adapter_up_panels = scatter_about(key_of[11], (ADAPTER_COUNT, ADAPTER_RANK, MODEL_WIDTH), ADAPTER_RANK ** -0.5, 0.75, ((0, 16), (2, 8)))
    return {"queries": queries, "fresh_key_value": fresh_key_value, "key_value_pool": key_value_pool, "request_page_table": request_page_table, "cached_length": cached_length, "move_holder_shard": move_holder_shard, "move_page_index": move_page_index, "request_adapter": request_adapter, "adapter_storage_slot": adapter_storage_slot, "output_projection": output_projection, "adapter_down_panels": adapter_down_panels, "adapter_up_panels": adapter_up_panels}


MASKED = -1e+30

def page_partials(query_head_rows, page_rows, live_counts):
    head_size_value = query_head_rows.shape[-1]
    key_part = page_rows[..., :head_size_value]
    value_part = page_rows[..., head_size_value:]
    scores = jnp.einsum('bkgd,bjtkd->bkgjt', query_head_rows, key_part) / math.sqrt(head_size_value)
    places = jnp.arange(page_rows.shape[2], dtype=jnp.int32)
    in_range = places[None, None, None, None, :] < live_counts[:, None, None, :, None]
    page_max = lax.optimization_barrier(jnp.max(jnp.where(in_range, scores, MASKED), axis=-1))
    weights = jnp.where(in_range, jnp.exp(scores - page_max[..., None]), 0.0).astype(jnp.bfloat16)
    widened = weights.astype(jnp.float32)
    page_sum = lax.optimization_barrier(jnp.sum(widened, axis=-1))
    page_out = jnp.einsum('bkgjt,bjtkd->bkgjd', widened, value_part)
    return (page_max, page_sum, page_out)

def merge_pages(page_max, page_sum, page_out, fresh_token_score, own_value):
    overall_max = jnp.maximum(lax.optimization_barrier(jnp.max(page_max, axis=-1)), fresh_token_score)
    rescale = jnp.exp(page_max - overall_max[..., None])
    own_weight = jnp.exp(fresh_token_score - overall_max)
    numerator = lax.optimization_barrier(jnp.sum(rescale[..., None] * page_out, axis=3)) + own_weight[..., None] * own_value[:, :, None, :]
    denominator = lax.optimization_barrier(jnp.sum(rescale * page_sum, axis=-1)) + own_weight
    return numerator / denominator[..., None]

def reference(queries, fresh_key_value, key_value_pool, request_page_table, cached_length, move_holder_shard, move_page_index, request_adapter, adapter_storage_slot, output_projection, adapter_down_panels, adapter_up_panels):
    holders = move_holder_shard[:, 0].reshape(N_REQ, MOVES)
    sources = holders * POOL + move_page_index.reshape(N_REQ, MOVES)
    own_pages = jnp.arange(N_REQ, dtype=jnp.int32)[:, None] * POOL + jnp.arange(POOL, dtype=jnp.int32)[None, :]
    extended = jnp.concatenate([own_pages, sources], axis=1).astype(jnp.int32)
    global_pages = jnp.take_along_axis(jnp.repeat(extended, REQ_DEV, axis=0), request_page_table.astype(jnp.int32), axis=1)
    request_slot = adapter_storage_slot[request_adapter]
    page_starts = jnp.arange(MAXP, dtype=jnp.int32) * PAGE
    live_counts = jnp.clip(cached_length[:, None] - page_starts[None, :], 0, PAGE)

    def one_shard(block):
        query_rows, fresh, page_ids, live, local_slot_indices = block
        query_head_rows = query_rows.astype(jnp.float32).reshape(REQ_DEV, KV_HEADS, QUERY_HEADS // KV_HEADS, HEAD_SIZE)
        page_rows = key_value_pool[page_ids].astype(jnp.float32)
        page_max, page_sum, page_out = page_partials(query_head_rows, page_rows, live)
        fresh_token_widened = fresh.astype(jnp.float32)
        fresh_token_score = jnp.einsum('jypf,jyf->jyp', query_head_rows, fresh_token_widened[..., :HEAD_SIZE]) / math.sqrt(HEAD_SIZE)
        attended = merge_pages(page_max, page_sum, page_out, fresh_token_score, fresh_token_widened[..., HEAD_SIZE:])
        attended = attended.reshape(REQ_DEV, QUERY_HEADS * HEAD_SIZE).astype(jnp.bfloat16)
        down_panel_chosen = adapter_down_panels[local_slot_indices].astype(jnp.float32)
        low_rank = jnp.einsum('rh,rhc->rc', attended.astype(jnp.float32), down_panel_chosen).astype(jnp.bfloat16)
        up_panel_chosen = adapter_up_panels[local_slot_indices].astype(jnp.float32)
        adapter_term = jnp.einsum('rc,rcd->rd', low_rank.astype(jnp.float32), up_panel_chosen)
        return (attended, adapter_term)
    blocks = (queries.reshape(N_REQ, REQ_DEV, QUERY_HEADS * HEAD_SIZE), fresh_key_value.reshape(N_REQ, REQ_DEV, KV_HEADS, 2 * HEAD_SIZE), global_pages.reshape(N_REQ, REQ_DEV, MAXP), live_counts.reshape(N_REQ, REQ_DEV, MAXP), request_slot.reshape(N_REQ, REQ_DEV))
    attended, adapter_term = lax.map(one_shard, blocks)
    projected = jnp.dot(attended.reshape(REQS, QUERY_HEADS * HEAD_SIZE), output_projection, preferred_element_type=jnp.float32)
    return (projected + adapter_term.reshape(REQS, MODEL_WIDTH)).astype(jnp.bfloat16)
```

```python
import functools
import math

import jax
import jax.numpy as jnp
from jax import lax
from jax.experimental import pallas as pl
from jax.experimental.pallas import tpu as pltpu
from jax.sharding import PartitionSpec as P

CAP = 4
MASKED = -1e30
F32 = jnp.float32
BF16 = jnp.bfloat16
META = 16


def iota(shape, dim):
    return lax.broadcasted_iota(jnp.int32, shape, dim)


def matmul(a, b):
    return lax.dot_general(a, b, (((1,), (0,)), ((), ())), preferred_element_type=F32)


def matmul_t(a, b):
    return lax.dot_general(a, b, (((1,), (1,)), ((), ())), preferred_element_type=F32)


def as_column(row):
    n = row.shape[1]
    return jnp.sum(jnp.where(iota((n, n), 0) == iota((n, n), 1), row, 0.0), axis=1, keepdims=True)


def as_row(column):
    n = column.shape[0]
    return jnp.sum(jnp.where(iota((n, n), 0) == iota((n, n), 1), column, 0.0), axis=0, keepdims=True)


def page_partial(q, page, live, head):
    scores = matmul_t(q, page[:, :head]) * (1.0 / math.sqrt(head))
    there = iota(scores.shape, 1) < live
    top = jnp.max(jnp.where(there, scores, MASKED), axis=1, keepdims=True)
    weights = jnp.where(there, jnp.exp(scores - top), 0.0).astype(BF16)
    total = jnp.sum(weights.astype(F32), axis=1, keepdims=True)
    return top, total, matmul(weights, page[:, head:])


def kernel(
    shards, tps,
    table, length, holder, index, adapter, storage, q, fresh, pool, w, down, up,
    out,
    pool_v, w_v, down_v, up_v, qmsg, qgot, rmsg, rgot, pick_v, pick_s, info_v, info_s,
    qown, qrh, own_live, fresh_v, o_u, m_u, l_u, att_f, att_b, att_all, psend, pgot,
    lsend, lgot, low_v, bsend, bgot,
    load_sem, w_sem, small_sem, q_sent, q_came, r_sent, r_came, a_sent, a_came,
    p_sent, p_came, l_sent, l_came, b_sent, b_came,
):
    me, tp = lax.axis_index("req"), lax.axis_index("tp")
    reqs, width = q.shape
    head = fresh.shape[1] // 2
    heads = width // head
    pages, page_len, _ = pool.shape
    moves = holder.shape[1]
    page_slots = table.shape[0]
    panels = storage.shape[1] // shards
    rank = down.shape[0] // panels
    columns = out.shape[1]
    qrows = CAP * heads

    pool_copy = pltpu.make_async_copy(pool, pool_v, load_sem.at[0])
    pool_copy.start()
    down_copy = pltpu.make_async_copy(down, down_v, load_sem.at[1])
    up_copy = pltpu.make_async_copy(up, up_v, load_sem.at[2])
    down_copy.start()
    up_copy.start()

    barrier = pltpu.get_barrier_semaphore()

    @pl.loop(1, shards)
    def _(off):
        pl.semaphore_signal(barrier, inc=1, device_id=(lax.rem(me + off, shards), tp), device_id_type=pl.DeviceIdType.MESH)

    @pl.loop(1, tps)
    def _(off):
        pl.semaphore_signal(barrier, inc=1, device_id=(me, lax.rem(tp + off, tps)), device_id_type=pl.DeviceIdType.MESH)

    def to_req(src, dst, sent, came, peer):
        return pltpu.make_async_remote_copy(
            src_ref=src, dst_ref=dst, send_sem=sent, recv_sem=came,
            device_id=(peer, tp), device_id_type=pl.DeviceIdType.MESH,
        )

    def to_tp(src, dst, sent, came, peer):
        return pltpu.make_async_remote_copy(
            src_ref=src, dst_ref=dst, send_sem=sent, recv_sem=came,
            device_id=(me, peer), device_id_type=pl.DeviceIdType.MESH,
        )

    hold_row = holder[...].astype(F32)
    hold_col = as_column(hold_row)
    earlier = iota((moves, moves), 1) < iota((moves, moves), 0)
    rank_col = jnp.sum(jnp.where(earlier & (hold_col == hold_row), 1.0, 0.0), axis=1, keepdims=True)
    slot_col = hold_col * CAP + rank_col
    slot_row = as_row(slot_col)
    index_col = as_column(index[...].astype(F32))
    lengths = length[...].astype(F32)
    request = iota((1, reqs), 1).astype(F32)
    move_req = jnp.zeros((moves, 1), F32)
    move_live = jnp.zeros((moves, 1), F32)
    own_req = jnp.zeros((pages, 1), F32)
    own_tokens = jnp.zeros((pages, 1), F32)
    for j in range(page_slots):
        entry = table[j : j + 1, :]
        live = jnp.clip(lengths - float(j * page_len), 0.0, float(page_len))
        hit = entry == pages + iota((moves, reqs), 0)
        mine = entry == iota((pages, reqs), 0)
        move_req += jnp.sum(jnp.where(hit, request, 0.0), axis=1, keepdims=True)
        move_live += jnp.sum(jnp.where(hit, live, 0.0), axis=1, keepdims=True)
        own_req += jnp.sum(jnp.where(mine, request, 0.0), axis=1, keepdims=True)
        own_tokens += jnp.sum(jnp.where(mine, live, 0.0), axis=1, keepdims=True)
        place = jnp.sum(jnp.where(hit, slot_col, 0.0), axis=0, keepdims=True).astype(jnp.int32)
        pick_v[j : j + 1, 0:reqs] = jnp.where(entry < pages, entry, pages + place)
    own_live[...] = jnp.broadcast_to(own_tokens, own_live.shape)

    stacked = jnp.concatenate([q[:, h * head : (h + 1) * head] for h in range(heads)], axis=0)
    hr = heads * reqs

    def spread(slot_of, rows, wanted):
        lane_req = lax.rem(iota((wanted.shape[0], hr), 1), reqs).astype(F32)
        choice = jnp.where(wanted == lane_req, 1.0, 0.0).astype(BF16)
        chosen = matmul(slot_of, choice)
        same_head = lax.rem(iota((rows, hr), 0), heads) == iota((rows, hr), 1) // reqs
        return matmul(jnp.where(same_head, chosen, 0.0).astype(BF16), stacked)

    slot_rows = shards * qrows
    to_slot = ((iota((slot_rows, moves), 0) // heads).astype(F32) == slot_row).astype(F32).astype(BF16)
    slot_q = spread(to_slot, slot_rows, move_req).astype(BF16)

    request_col = as_column(adapter[...].astype(F32))
    slots = storage.shape[1]
    request_slot = jnp.sum(
        jnp.where(request_col == iota((reqs, slots), 1).astype(F32), storage[...].astype(F32), 0.0), axis=1, keepdims=True
    )
    lane = iota((moves, 128), 1).astype(F32)
    asked = jnp.where(lane == rank_col, index_col, 0.0) + jnp.where(lane == rank_col + CAP, move_live, 0.0)
    by_holder = (iota((shards, moves), 0).astype(F32) == hold_row).astype(F32).astype(BF16)
    ask = matmul(by_holder, asked.astype(BF16))
    first = iota((META, 128), 0) == 0
    upper = iota((META, 128), 1) >= 64
    for d in range(shards):
        qmsg[d, 0:qrows, :] = slot_q[d * qrows : (d + 1) * qrows]
        qmsg[d, qrows : qrows + META, :] = jnp.where(
            upper, request_slot, jnp.where(first, ask[d : d + 1, :], 0.0)
        ).astype(BF16)

    pl.semaphore_wait(barrier, shards - 1 + tps - 1)

    def ask_copy(peer, slot):
        return to_req(qmsg.at[peer], qgot.at[slot], q_sent.at[peer], q_came.at[slot], peer)

    @pl.loop(1, shards)
    def _(off):
        ask_copy(lax.rem(me + off, shards), me).start()

    qgot[pl.ds(me, 1)] = qmsg[pl.ds(me, 1)]

    own_rows = pages * heads
    to_page = ((iota((own_rows, pages), 0) // heads) == iota((own_rows, pages), 1)).astype(F32).astype(BF16)
    qown[...] = spread(to_page, own_rows, own_req).reshape(pages, heads, head)
    swap = (iota((hr, hr), 0) // heads == lax.rem(iota((hr, hr), 1), reqs)) & (
        lax.rem(iota((hr, hr), 0), heads) == iota((hr, hr), 1) // reqs
    )
    qrh[...] = matmul(swap.astype(F32).astype(BF16), stacked).reshape(reqs, heads, head)
    fresh_v[...] = fresh[...].astype(F32)
    pick_copy = pltpu.make_async_copy(pick_v, pick_s, small_sem.at[0])
    pick_copy.start()

    pool_copy.wait()
    w_copies = [
        pltpu.make_async_copy(w.at[:, pl.ds(c * columns, columns)], w_v.at[c], w_sem.at[c]) for c in range(tps)
    ]
    for copy in w_copies:
        copy.start()

    together = 4

    @pl.loop(0, pages // together)
    def _(group):
        for k in range(together):
            i = group * together + k
            top, total, part = page_partial(qown[i].astype(BF16), pool_v[i], own_live[pl.ds(i, 1), 0:1].astype(jnp.int32), head)
            o_u[i] = part
            m_u[i] = jnp.broadcast_to(top, (heads, head))
            l_u[i] = jnp.broadcast_to(total, (heads, head))

    @pl.loop(1, shards)
    def _(off):
        source = lax.rem(me + shards - off, shards)
        ask_copy(source, source).wait_recv()

    wanted = jnp.concatenate([qgot[s, qrows : qrows + META, :][0:1].astype(F32) for s in range(shards)], axis=0)
    info_v[...] = wanted.astype(jnp.int32)
    info_copy = pltpu.make_async_copy(info_v, info_s, small_sem.at[1])
    info_copy.start()
    info_copy.wait()

    block = iota((heads, 128), 1) // 32
    piece = lax.rem(iota((heads, 128), 1), 32) // 8

    def serve(source):
        queries = qgot[source, 0:qrows, :].astype(F32)
        tops = jnp.zeros((heads, 128), F32)
        totals = jnp.zeros((heads, 128), F32)
        parts = []
        for c in range(CAP):
            page = pool_v[jnp.clip(info_s[source, c], 0, pages - 1)]
            top, total, part = page_partial(
                queries[c * heads : (c + 1) * heads].astype(BF16), page, info_s[source, CAP + c], head
            )
            tops = jnp.where(block == c, top, tops)
            totals = jnp.where(block == c, total, totals)
            parts.append(part)
        high = tops.astype(BF16).astype(F32)
        rest = tops - high
        middle = rest.astype(BF16).astype(F32)
        sum_high = totals.astype(BF16).astype(F32)
        packed = jnp.where(piece == 0, high, jnp.where(piece == 1, middle, jnp.where(piece == 2, rest - middle, sum_high)))
        rmsg[source, 0:qrows, :] = jnp.concatenate(parts, axis=0).astype(BF16)
        rmsg[source, qrows : qrows + META, :] = jnp.concatenate([packed, totals - sum_high], axis=0).astype(BF16)

    def part_copy(peer, slot):
        return to_req(rmsg.at[peer], rgot.at[slot], r_sent.at[peer], r_came.at[slot], peer)

    @pl.loop(1, shards)
    def _(off):
        source = lax.rem(me + off, shards)
        serve(source)
        part_copy(source, me).start()

    serve(me)
    rgot[pl.ds(me, 1)] = rmsg[pl.ds(me, 1)]

    def unpack(source):
        parts = rgot[source, 0:qrows, :].astype(F32)
        tail = rgot[source, qrows : qrows + META, :].astype(F32)
        packed = tail[0:heads]
        tops = packed + pltpu.roll(packed, 120, 1) + pltpu.roll(packed, 112, 1)
        totals = packed + tail[heads : 2 * heads]
        for c in range(CAP):
            unit = pages + source * CAP + c
            o_u[unit] = parts[c * heads : (c + 1) * heads]
            m_u[unit] = jnp.broadcast_to(tops[:, c * 32 : c * 32 + 1], (heads, head))
            l_u[unit] = jnp.broadcast_to(totals[:, c * 32 + 24 : c * 32 + 25], (heads, head))

    unpack(me)

    @pl.loop(1, shards)
    def _(off):
        source = lax.rem(me + shards - off, shards)
        part_copy(source, source).wait_recv()
        unpack(source)

    pick_copy.wait()

    @pl.loop(0, reqs // together)
    def _(group):
        for k in range(together):
            r = group * together + k
            units = [jnp.clip(pick_s[j, r], 0, o_u.shape[0] - 1) for j in range(page_slots)]
            tops = [m_u[u] for u in units]
            new = fresh_v[pl.ds(r, 1), :]
            own = jnp.sum(qrh[r] * new[:, :head], axis=1, keepdims=True) * (1.0 / math.sqrt(head))
            overall = functools.reduce(jnp.maximum, tops)
            overall = jnp.maximum(overall, own)
            own_weight = jnp.exp(own - overall)
            above = own_weight * new[:, head:]
            below = own_weight
            for u, top in zip(units, tops):
                scale = jnp.exp(top - overall)
                above += scale * o_u[u]
                below += scale * l_u[u]
            att_f[r] = above / below

    att_b[...] = jnp.concatenate([att_f[:, h, :] for h in range(heads)], axis=1).astype(BF16)

    def att_copy(peer, slot):
        return to_req(att_b, att_all.at[slot], a_sent.at[peer], a_came.at[slot], peer)

    @pl.loop(1, shards)
    def _(off):
        att_copy(lax.rem(me + off, shards), me).start()

    att_all[pl.ds(me, 1)] = att_b[...][None]

    for copy in w_copies:
        copy.wait()

    def p_copy(peer, slot):
        return to_tp(psend.at[peer], pgot.at[slot], p_sent.at[peer], p_came.at[slot], peer)

    @pl.loop(1, tps)
    def _(off):
        peer = lax.rem(tp + off, tps)
        psend[peer] = matmul(att_b[...], w_v[peer]).astype(BF16)
        p_copy(peer, tp).start()

    total = matmul(att_b[...], w_v[tp])

    down_copy.wait()
    up_copy.wait()

    @pl.loop(1, shards)
    def _(off):
        source = lax.rem(me + shards - off, shards)
        att_copy(source, source).wait_recv()

    rows = shards * reqs
    half = rows // 2
    tags = jnp.concatenate([qgot[s, qrows : qrows + META, :] for s in range(shards)], axis=0).astype(F32)
    panel = tags[:, 64:65] - (me * panels).astype(F32)
    here = (iota((rows, panels * rank), 1) // rank).astype(F32) == panel
    low = matmul_t(att_all[...].reshape(rows, width), down_v[...])
    low = jnp.where(here, low, 0.0)
    low = low[:, :128] + low[:, 128:]
    low = low + pltpu.roll(low, 64, 1)
    left = iota((half, 128), 1) < 64
    lsend[...] = jnp.where(left, low[:half], low[half:]).astype(BF16)

    def l_copy(peer, slot):
        return to_tp(lsend, lgot.at[slot], l_sent.at[peer], l_came.at[slot], peer)

    @pl.loop(1, tps)
    def _(off):
        l_copy(lax.rem(tp + off, tps), tp).start()

    lgot[pl.ds(tp, 1)] = lsend[...][None]

    @pl.loop(1, tps)
    def _(off):
        source = lax.rem(tp + tps - off, tps)
        l_copy(source, source).wait_recv()

    whole = jnp.sum(lgot[...].astype(F32), axis=0).astype(BF16).astype(F32)
    turned = pltpu.roll(whole, 64, 1)
    both = jnp.concatenate([jnp.where(left, whole, turned), jnp.where(left, turned, whole)], axis=0)
    low_v[...] = jnp.where(here, jnp.concatenate([both, both], axis=1), 0.0).astype(BF16)

    chunk = 4 * reqs

    @pl.loop(0, rows // chunk)
    def _(c):
        term = matmul(low_v[pl.ds(pl.multiple_of(c * chunk, chunk), chunk), :], up_v[...])
        bsend[pl.ds(c * 4, 4)] = term.astype(BF16).reshape(4, reqs, columns)

    def b_copy(peer, slot):
        return to_req(bsend.at[peer], bgot.at[slot], b_sent.at[peer], b_came.at[slot], peer)

    @pl.loop(1, shards)
    def _(off):
        b_copy(lax.rem(me + off, shards), me).start()

    bgot[pl.ds(me, 1)] = bsend[pl.ds(me, 1)]

    @pl.loop(1, tps)
    def _(off):
        source = lax.rem(tp + tps - off, tps)
        p_copy(source, source).wait_recv()

    pgot[pl.ds(tp, 1)] = jnp.zeros((1, reqs, columns), BF16)
    total += jnp.sum(pgot[...].astype(F32), axis=0)

    @pl.loop(1, shards)
    def _(off):
        source = lax.rem(me + shards - off, shards)
        b_copy(source, source).wait_recv()

    total += jnp.sum(bgot[...].astype(F32), axis=0)
    out[...] = total.astype(BF16)

    @pl.loop(1, shards)
    def _(off):
        peer = lax.rem(me + off, shards)
        ask_copy(peer, me).wait_send()
        part_copy(peer, me).wait_send()
        att_copy(peer, me).wait_send()
        b_copy(peer, me).wait_send()

    @pl.loop(1, tps)
    def _(off):
        peer = lax.rem(tp + off, tps)
        p_copy(peer, tp).wait_send()
        l_copy(peer, tp).wait_send()


def local(
    shards, tps,
    queries, fresh_key_value, key_value_pool, request_page_table, cached_length, move_holder_shard, move_page_index,
    request_adapter, adapter_storage_slot, output_projection, adapter_down_panels, adapter_up_panels,
):
    reqs, width = queries.shape
    pages, page_len, _, kv = key_value_pool.shape
    head = kv // 2
    heads = width // head
    panels, _, rank = adapter_down_panels.shape
    columns = output_projection.shape[1] // tps
    qrows = CAP * heads
    units = pages + shards * CAP
    rows = shards * reqs
    dma = pltpu.SemaphoreType.DMA
    small = pl.BlockSpec(memory_space=pltpu.VMEM)
    large = pl.BlockSpec(memory_space=pl.ANY)
    return pl.pallas_call(
        functools.partial(kernel, shards, tps),
        out_shape=jax.ShapeDtypeStruct((reqs, columns), BF16),
        in_specs=[small] * 8 + [large] * 4,
        out_specs=small,
        scratch_shapes=[
            pltpu.VMEM((pages, page_len, kv), BF16),
            pltpu.VMEM((tps, width, columns), BF16),
            pltpu.VMEM((panels * rank, width), BF16),
            pltpu.VMEM((panels * rank, columns), BF16),
            pltpu.VMEM((shards, qrows + META, head), BF16),
            pltpu.VMEM((shards, qrows + META, head), BF16),
            pltpu.VMEM((shards, qrows + META, head), BF16),
            pltpu.VMEM((shards, qrows + META, head), BF16),
            pltpu.VMEM((8, 128), jnp.int32),
            pltpu.SMEM((8, 128), jnp.int32),
            pltpu.VMEM((shards, 128), jnp.int32),
            pltpu.SMEM((shards, 128), jnp.int32),
            pltpu.VMEM((pages, heads, head), F32),
            pltpu.VMEM((reqs, heads, head), F32),
            pltpu.VMEM((pages, 128), F32),
            pltpu.VMEM((reqs, kv), F32),
            pltpu.VMEM((units, heads, head), F32),
            pltpu.VMEM((units, heads, head), F32),
            pltpu.VMEM((units, heads, head), F32),
            pltpu.VMEM((reqs, heads, head), F32),
            pltpu.VMEM((reqs, width), BF16),
            pltpu.VMEM((shards, reqs, width), BF16),
            pltpu.VMEM((tps, reqs, columns), BF16),
            pltpu.VMEM((tps, reqs, columns), BF16),
            pltpu.VMEM((rows // 2, 128), BF16),
            pltpu.VMEM((tps, rows // 2, 128), BF16),
            pltpu.VMEM((rows, panels * rank), BF16),
            pltpu.VMEM((shards, reqs, columns), BF16),
            pltpu.VMEM((shards, reqs, columns), BF16),
            dma((3,)), dma((tps,)), dma((2,)),
            dma((shards,)), dma((shards,)), dma((shards,)), dma((shards,)), dma((shards,)), dma((shards,)),
            dma((tps,)), dma((tps,)), dma((tps,)), dma((tps,)),
            dma((shards,)), dma((shards,)),
        ],
        compiler_params=pltpu.CompilerParams(
            collective_id=0, has_side_effects=True, vmem_limit_bytes=48 * 1024 * 1024
        ),
    )(
        request_page_table.T,
        cached_length.reshape(1, -1),
        move_holder_shard.reshape(1, -1),
        move_page_index.reshape(1, -1),
        request_adapter.reshape(1, -1),
        adapter_storage_slot.reshape(1, -1),
        queries,
        fresh_key_value.reshape(reqs, kv),
        key_value_pool.reshape(pages, page_len, kv),
        output_projection,
        jnp.swapaxes(adapter_down_panels, 1, 2).reshape(panels * rank, width),
        adapter_up_panels.reshape(panels * rank, columns),
    )


def solution(mesh):
    shards, tps = mesh.shape["req"], mesh.shape["tp"]
    return jax.shard_map(
        functools.partial(local, shards, tps),
        mesh=mesh,
        in_specs=(
            P("req", "tp"),
            P("req", "tp", None),
            P("req", None, "tp", None),
            P("req", None),
            P("req"),
            P("req", None),
            P("req"),
            P("req"),
            P(),
            P("tp", None),
            P("req", "tp", None),
            P("req", None, "tp"),
        ),
        out_specs=P("req", "tp"),
        check_vma=False,
    )
```

```python
import functools
import math

import jax
import jax.numpy as jnp
from jax import lax
from jax.experimental import pallas as pl
from jax.experimental.pallas import tpu as pltpu
from jax.sharding import PartitionSpec as P

CAP = 4
MASKED = -1e30
F32 = jnp.float32
BF16 = jnp.bfloat16
META = 16


def iota(shape, dim):
    return lax.broadcasted_iota(jnp.int32, shape, dim)


def matmul(a, b):
    return lax.dot_general(a, b, (((1,), (0,)), ((), ())), preferred_element_type=F32)


def matmul_t(a, b):
    return lax.dot_general(a, b, (((1,), (1,)), ((), ())), preferred_element_type=F32)


def as_column(row):
    n = row.shape[1]
    return jnp.sum(jnp.where(iota((n, n), 0) == iota((n, n), 1), row, 0.0), axis=1, keepdims=True)


def as_row(column):
    n = column.shape[0]
    return jnp.sum(jnp.where(iota((n, n), 0) == iota((n, n), 1), column, 0.0), axis=0, keepdims=True)


def page_partials(queries, pages, live, head):
    heads = queries.shape[0] // len(pages)
    rows = [slice(k * heads, (k + 1) * heads) for k in range(len(pages))]
    scores = [matmul_t(queries[rows[k]].astype(BF16), page[:, :head]) for k, page in enumerate(pages)]
    scores = jnp.concatenate(scores, axis=0) * (1.0 / math.sqrt(head))
    there = iota(scores.shape, 1).astype(F32) < live
    top = jnp.max(jnp.where(there, scores, MASKED), axis=1, keepdims=True)
    weights = jnp.where(there, jnp.exp(scores - top), 0.0).astype(BF16).astype(F32)
    total = jnp.sum(weights, axis=1, keepdims=True)
    parts = [matmul(weights[rows[k]].astype(BF16), page[:, head:]) for k, page in enumerate(pages)]
    return top, total, jnp.concatenate(parts, axis=0)


def kernel(
    shards, tps,
    table_in, length_in, holder_in, index_in, adapter_in, storage_in, q_in, fresh_in, pool, w, down, up,
    out,
    table, length, holder, index, adapter, storage, q, fresh,
    pool_v, w_v, down_v, up_v, qmsg, qgot, rmsg, rgot, pick_v, pick_s, info_v, info_s,
    qown, qrh, own_live, fresh_v, o_u, m_u, l_u, att_f, att_b, att_all, psend, pgot,
    lsend, lgot, low_v, bsend, bgot,
    in_sem, load_sem, w_sem, small_sem, q_sent, q_came, r_sent, r_came, a_sent, a_came,
    p_sent, p_came, l_sent, l_came, b_sent, b_came,
):
    me, tp = lax.axis_index("req"), lax.axis_index("tp")
    reqs, width = q.shape
    head = fresh.shape[1] // 2
    heads = width // head
    pages, page_len, _ = pool.shape
    moves = holder.shape[1]
    page_slots = table.shape[0]
    panels = storage.shape[1] // shards
    rank = down.shape[0] // panels
    columns = out.shape[1]
    qrows = CAP * heads

    small_copies = [
        pltpu.make_async_copy(source, here, in_sem.at[n])
        for n, (source, here) in enumerate(
            (
                (holder_in, holder), (index_in, index), (table_in, table), (length_in, length),
                (q_in, q), (adapter_in, adapter), (storage_in, storage), (fresh_in, fresh),
            )
        )
    ]
    for copy in small_copies:
        copy.start()
    pool_copy = pltpu.make_async_copy(pool, pool_v, load_sem.at[0])
    pool_copy.start()
    down_copy = pltpu.make_async_copy(down, down_v, load_sem.at[1])
    up_copy = pltpu.make_async_copy(up, up_v, load_sem.at[2])
    down_copy.start()
    up_copy.start()

    barrier = pltpu.get_barrier_semaphore()

    @pl.loop(1, shards)
    def _(off):
        pl.semaphore_signal(barrier, inc=1, device_id=(lax.rem(me + off, shards), tp), device_id_type=pl.DeviceIdType.MESH)

    @pl.loop(1, tps)
    def _(off):
        pl.semaphore_signal(barrier, inc=1, device_id=(me, lax.rem(tp + off, tps)), device_id_type=pl.DeviceIdType.MESH)

    def to_req(src, dst, sent, came, peer):
        return pltpu.make_async_remote_copy(
            src_ref=src, dst_ref=dst, send_sem=sent, recv_sem=came,
            device_id=(peer, tp), device_id_type=pl.DeviceIdType.MESH,
        )

    def to_tp(src, dst, sent, came, peer):
        return pltpu.make_async_remote_copy(
            src_ref=src, dst_ref=dst, send_sem=sent, recv_sem=came,
            device_id=(me, peer), device_id_type=pl.DeviceIdType.MESH,
        )

    for copy in small_copies:
        copy.wait()

    hold_row = holder[...].astype(F32)
    hold_col = as_column(hold_row)
    earlier = iota((moves, moves), 1) < iota((moves, moves), 0)
    rank_col = jnp.sum(jnp.where(earlier & (hold_col == hold_row), 1.0, 0.0), axis=1, keepdims=True)
    slot_col = hold_col * CAP + rank_col
    slot_row = as_row(slot_col)
    index_col = as_column(index[...].astype(F32))
    lengths = length[...].astype(F32)
    request = iota((1, reqs), 1).astype(F32)
    move_req = jnp.zeros((moves, 1), F32)
    move_live = jnp.zeros((moves, 1), F32)
    own_req = jnp.zeros((pages, 1), F32)
    own_tokens = jnp.zeros((pages, 1), F32)
    for j in range(page_slots):
        entry = table[j : j + 1, :]
        live = jnp.clip(lengths - float(j * page_len), 0.0, float(page_len))
        hit = entry == pages + iota((moves, reqs), 0)
        mine = entry == iota((pages, reqs), 0)
        move_req += jnp.sum(jnp.where(hit, request, 0.0), axis=1, keepdims=True)
        move_live += jnp.sum(jnp.where(hit, live, 0.0), axis=1, keepdims=True)
        own_req += jnp.sum(jnp.where(mine, request, 0.0), axis=1, keepdims=True)
        own_tokens += jnp.sum(jnp.where(mine, live, 0.0), axis=1, keepdims=True)
        place = jnp.sum(jnp.where(hit, slot_col, 0.0), axis=0, keepdims=True).astype(jnp.int32)
        pick_v[j : j + 1, 0:reqs] = jnp.where(entry < pages, entry, pages + place)

    stacked = jnp.concatenate([q[:, h * head : (h + 1) * head] for h in range(heads)], axis=0)
    hr = heads * reqs

    def spread(slot_of, rows, wanted):
        lane_req = lax.rem(iota((wanted.shape[0], hr), 1), reqs).astype(F32)
        choice = jnp.where(wanted == lane_req, 1.0, 0.0).astype(BF16)
        chosen = matmul(slot_of, choice)
        same_head = lax.rem(iota((rows, hr), 0), heads) == iota((rows, hr), 1) // reqs
        return matmul(jnp.where(same_head, chosen, 0.0).astype(BF16), stacked)

    slot_rows = shards * qrows
    to_slot = ((iota((slot_rows, moves), 0) // heads).astype(F32) == slot_row).astype(F32).astype(BF16)
    slot_q = spread(to_slot, slot_rows, move_req).astype(BF16)

    request_col = as_column(adapter[...].astype(F32))
    slots = storage.shape[1]
    request_slot = jnp.sum(
        jnp.where(request_col == iota((reqs, slots), 1).astype(F32), storage[...].astype(F32), 0.0), axis=1, keepdims=True
    )
    lane = iota((moves, 128), 1).astype(F32)
    asked = jnp.where(lane == rank_col, index_col, 0.0) + jnp.where(lane == rank_col + CAP, move_live, 0.0)
    by_holder = (iota((shards, moves), 0).astype(F32) == hold_row).astype(F32).astype(BF16)
    ask = matmul(by_holder, asked.astype(BF16))
    first = iota((META, 128), 0) == 0
    upper = iota((META, 128), 1) >= 64
    for d in range(shards):
        qmsg[d, 0:qrows, :] = slot_q[d * qrows : (d + 1) * qrows]
        qmsg[d, qrows : qrows + META, :] = jnp.where(
            upper, request_slot, jnp.where(first, ask[d : d + 1, :], 0.0)
        ).astype(BF16)

    pl.semaphore_wait(barrier, shards - 1 + tps - 1)

    def ask_copy(peer, slot):
        return to_req(qmsg.at[peer], qgot.at[slot], q_sent.at[peer], q_came.at[slot], peer)

    @pl.loop(1, shards)
    def _(off):
        ask_copy(lax.rem(me + off, shards), me).start()

    qgot[pl.ds(me, 1)] = qmsg[pl.ds(me, 1)]

    own_rows = pages * heads
    to_page = ((iota((own_rows, pages), 0) // heads) == iota((own_rows, pages), 1)).astype(F32).astype(BF16)
    qown[...] = spread(to_page, own_rows, own_req)
    own_live[...] = matmul(to_page, jnp.broadcast_to(own_tokens, (pages, 128)).astype(BF16))
    swap = (iota((hr, hr), 0) // heads == lax.rem(iota((hr, hr), 1), reqs)) & (
        lax.rem(iota((hr, hr), 0), heads) == iota((hr, hr), 1) // reqs
    )
    qrh[...] = matmul(swap.astype(F32).astype(BF16), stacked).reshape(reqs, heads, head)
    fresh_v[...] = fresh[...].astype(F32)
    pick_copy = pltpu.make_async_copy(pick_v, pick_s, small_sem.at[0])
    pick_copy.start()

    pool_copy.wait()
    w_copies = [
        pltpu.make_async_copy(w.at[:, pl.ds(c * columns, columns)], w_v.at[c], w_sem.at[c]) for c in range(tps)
    ]
    for copy in w_copies:
        copy.start()

    batch = 16

    @pl.loop(0, pages // batch)
    def _(group):
        rows = pl.ds(pl.multiple_of(group * batch * heads, batch * heads), batch * heads)
        units = pl.ds(group * batch, batch)
        top, total, part = page_partials(
            qown[rows, :], [pool_v.at[group * batch + k] for k in range(batch)], own_live[rows, 0:1], head
        )
        o_u[units] = part.reshape(batch, heads, head)
        m_u[units] = jnp.broadcast_to(top, part.shape).reshape(batch, heads, head)
        l_u[units] = jnp.broadcast_to(total, part.shape).reshape(batch, heads, head)

    @pl.loop(1, shards)
    def _(off):
        source = lax.rem(me + shards - off, shards)
        ask_copy(source, source).wait_recv()

    wanted = jnp.concatenate([qgot[s, qrows : qrows + META, :][0:1].astype(F32) for s in range(shards)], axis=0)
    info_v[...] = wanted.astype(jnp.int32)
    info_copy = pltpu.make_async_copy(info_v, info_s, small_sem.at[1])
    info_copy.start()
    info_copy.wait()

    block = iota((heads, 128), 1) // 32
    piece = lax.rem(iota((heads, 128), 1), 32) // 8

    def part_copy(peer, slot):
        return to_req(rmsg.at[peer], rgot.at[slot], r_sent.at[peer], r_came.at[slot], peer)

    group_of = 4

    @pl.loop(0, shards // group_of)
    def _(group):
        sources = [lax.rem(me + 1 + group * group_of + k, shards) for k in range(group_of)]
        queries = jnp.concatenate([qgot[source, 0:qrows, :].astype(F32) for source in sources], axis=0)
        picked, live = [], []
        for source in sources:
            for c in range(CAP):
                picked.append(pool_v.at[jnp.clip(info_s[source, c], 0, pages - 1)])
                live.append(jnp.full((heads, 1), info_s[source, CAP + c], jnp.int32))
        top, total, part = page_partials(queries, picked, jnp.concatenate(live, axis=0).astype(F32), head)
        bodies, tails = [], []
        for k in range(group_of):
            tops = jnp.zeros((heads, 128), F32)
            totals = jnp.zeros((heads, 128), F32)
            for c in range(CAP):
                rows = slice((k * CAP + c) * heads, (k * CAP + c + 1) * heads)
                tops = jnp.where(block == c, top[rows], tops)
                totals = jnp.where(block == c, total[rows], totals)
            high = tops.astype(BF16).astype(F32)
            rest = tops - high
            middle = rest.astype(BF16).astype(F32)
            sum_high = totals.astype(BF16).astype(F32)
            packed = jnp.where(
                piece == 0, high, jnp.where(piece == 1, middle, jnp.where(piece == 2, rest - middle, sum_high))
            )
            bodies.append(part[k * qrows : (k + 1) * qrows].astype(BF16))
            tails.append(jnp.concatenate([packed, totals - sum_high], axis=0).astype(BF16))
        for source, body, tail in zip(sources, bodies, tails):
            rmsg[source, 0:qrows, :] = body
            rmsg[source, qrows : qrows + META, :] = tail
        for source in sources:

            @pl.when(source != me)
            def _():
                part_copy(source, me).start()

    rgot[pl.ds(me, 1)] = rmsg[pl.ds(me, 1)]

    @pl.loop(0, shards // group_of)
    def _(group):
        sources = [lax.rem(me + 2 * shards - 1 - group * group_of - k, shards) for k in range(group_of)]
        for source in sources:

            @pl.when(source != me)
            def _():
                part_copy(source, source).wait_recv()

        found = []
        for source in sources:
            part = rgot[source, 0:qrows, :].astype(F32)
            tail = rgot[source, qrows : qrows + META, :].astype(F32)
            packed = tail[0:heads]
            tops = packed + pltpu.roll(packed, 120, 1) + pltpu.roll(packed, 112, 1)
            totals = packed + tail[heads : 2 * heads]
            top = jnp.concatenate([tops[:, c * 32 : c * 32 + 1] for c in range(CAP)], axis=0)
            total = jnp.concatenate([totals[:, c * 32 + 24 : c * 32 + 25] for c in range(CAP)], axis=0)
            found.append((part, jnp.broadcast_to(top, part.shape), jnp.broadcast_to(total, part.shape)))
        for source, values in zip(sources, found):
            units = pl.ds(pages + source * CAP, CAP)
            for kept, value in zip((o_u, m_u, l_u), values):
                kept[units] = value.reshape(CAP, heads, head)

    pick_copy.wait()

    @pl.loop(0, reqs // group_of)
    def _(group):
        merged = []
        for k in range(group_of):
            r = group * group_of + k
            units = [jnp.clip(pick_s[j, r], 0, o_u.shape[0] - 1) for j in range(page_slots)]
            tops = [m_u[u] for u in units]
            new = fresh_v[pl.ds(r, 1), :]
            own = jnp.sum(qrh[r] * new[:, :head], axis=1, keepdims=True) * (1.0 / math.sqrt(head))
            overall = jnp.maximum(functools.reduce(jnp.maximum, tops), own)
            own_weight = jnp.exp(own - overall)
            above = own_weight * new[:, head:]
            below = own_weight
            for u, top in zip(units, tops):
                scale = jnp.exp(top - overall)
                above += scale * o_u[u]
                below += scale * l_u[u]
            merged.append((above / below)[None])
        att_f[pl.ds(group * group_of, group_of)] = jnp.concatenate(merged, axis=0)

    att_b[...] = jnp.concatenate([att_f[:, h, :] for h in range(heads)], axis=1).astype(BF16)

    def att_copy(peer, slot):
        return to_req(att_b, att_all.at[slot], a_sent.at[peer], a_came.at[slot], peer)

    @pl.loop(1, shards)
    def _(off):
        att_copy(lax.rem(me + off, shards), me).start()

    att_all[pl.ds(me, 1)] = att_b[...][None]

    for copy in w_copies:
        copy.wait()

    def p_copy(peer, slot):
        return to_tp(psend.at[peer], pgot.at[slot], p_sent.at[peer], p_came.at[slot], peer)

    @pl.loop(1, tps)
    def _(off):
        peer = lax.rem(tp + off, tps)
        psend[peer] = matmul(att_b[...], w_v[peer]).astype(BF16)
        p_copy(peer, tp).start()

    total = matmul(att_b[...], w_v[tp])

    down_copy.wait()
    up_copy.wait()

    @pl.loop(1, shards)
    def _(off):
        source = lax.rem(me + shards - off, shards)
        att_copy(source, source).wait_recv()

    rows = shards * reqs
    half = rows // 2
    tags = jnp.concatenate([qgot[s, qrows : qrows + META, :] for s in range(shards)], axis=0).astype(F32)
    panel = tags[:, 64:65] - (me * panels).astype(F32)
    here = (iota((rows, panels * rank), 1) // rank).astype(F32) == panel
    low = matmul_t(att_all[...].reshape(rows, width), down_v[...])
    low = jnp.where(here, low, 0.0)
    low = low[:, :128] + low[:, 128:]
    low = low + pltpu.roll(low, 64, 1)
    left = iota((half, 128), 1) < 64
    lsend[...] = jnp.where(left, low[:half], low[half:]).astype(BF16)

    def l_copy(peer, slot):
        return to_tp(lsend, lgot.at[slot], l_sent.at[peer], l_came.at[slot], peer)

    @pl.loop(1, tps)
    def _(off):
        l_copy(lax.rem(tp + off, tps), tp).start()

    lgot[pl.ds(tp, 1)] = lsend[...][None]

    @pl.loop(1, tps)
    def _(off):
        source = lax.rem(tp + tps - off, tps)
        l_copy(source, source).wait_recv()

    whole = jnp.sum(lgot[...].astype(F32), axis=0).astype(BF16).astype(F32)
    turned = pltpu.roll(whole, 64, 1)
    both = jnp.concatenate([jnp.where(left, whole, turned), jnp.where(left, turned, whole)], axis=0)
    low_v[...] = jnp.where(here, jnp.concatenate([both, both], axis=1), 0.0).astype(BF16)

    chunk = 4 * reqs

    @pl.loop(0, rows // chunk)
    def _(c):
        term = matmul(low_v[pl.ds(pl.multiple_of(c * chunk, chunk), chunk), :], up_v[...])
        bsend[pl.ds(c * 4, 4)] = term.astype(BF16).reshape(4, reqs, columns)

    def b_copy(peer, slot):
        return to_req(bsend.at[peer], bgot.at[slot], b_sent.at[peer], b_came.at[slot], peer)

    @pl.loop(1, shards)
    def _(off):
        b_copy(lax.rem(me + off, shards), me).start()

    bgot[pl.ds(me, 1)] = bsend[pl.ds(me, 1)]

    @pl.loop(1, tps)
    def _(off):
        source = lax.rem(tp + tps - off, tps)
        p_copy(source, source).wait_recv()

    pgot[pl.ds(tp, 1)] = jnp.zeros((1, reqs, columns), BF16)
    total += jnp.sum(pgot[...].astype(F32), axis=0)

    @pl.loop(1, shards)
    def _(off):
        source = lax.rem(me + shards - off, shards)
        b_copy(source, source).wait_recv()

    total += jnp.sum(bgot[...].astype(F32), axis=0)
    out[...] = total.astype(BF16)

    @pl.loop(1, shards)
    def _(off):
        peer = lax.rem(me + off, shards)
        ask_copy(peer, me).wait_send()
        part_copy(peer, me).wait_send()
        att_copy(peer, me).wait_send()
        b_copy(peer, me).wait_send()

    @pl.loop(1, tps)
    def _(off):
        peer = lax.rem(tp + off, tps)
        p_copy(peer, tp).wait_send()
        l_copy(peer, tp).wait_send()


def local(
    shards, tps,
    queries, fresh_key_value, key_value_pool, request_page_table, cached_length, move_holder_shard, move_page_index,
    request_adapter, adapter_storage_slot, output_projection, adapter_down_panels, adapter_up_panels,
):
    reqs, width = queries.shape
    pages, page_len, _, kv = key_value_pool.shape
    head = kv // 2
    heads = width // head
    panels, _, rank = adapter_down_panels.shape
    columns = output_projection.shape[1] // tps
    qrows = CAP * heads
    units = pages + shards * CAP
    rows = shards * reqs
    dma = pltpu.SemaphoreType.DMA
    small = pl.BlockSpec(memory_space=pltpu.VMEM)
    large = pl.BlockSpec(memory_space=pl.ANY)
    return pl.pallas_call(
        functools.partial(kernel, shards, tps),
        out_shape=jax.ShapeDtypeStruct((reqs, columns), BF16),
        in_specs=[large] * 12,
        out_specs=small,
        scratch_shapes=[
            pltpu.VMEM(request_page_table.shape[::-1], jnp.int32),
            pltpu.VMEM((1, reqs), jnp.int32),
            pltpu.VMEM((1, move_holder_shard.shape[0]), jnp.int32),
            pltpu.VMEM((1, move_holder_shard.shape[0]), jnp.int32),
            pltpu.VMEM((1, reqs), jnp.int32),
            pltpu.VMEM((1, adapter_storage_slot.shape[0]), jnp.int32),
            pltpu.VMEM((reqs, width), BF16),
            pltpu.VMEM((reqs, kv), BF16),
            pltpu.VMEM((pages, page_len, kv), BF16),
            pltpu.VMEM((tps, width, columns), BF16),
            pltpu.VMEM((panels * rank, width), BF16),
            pltpu.VMEM((panels * rank, columns), BF16),
            pltpu.VMEM((shards, qrows + META, head), BF16),
            pltpu.VMEM((shards, qrows + META, head), BF16),
            pltpu.VMEM((shards, qrows + META, head), BF16),
            pltpu.VMEM((shards, qrows + META, head), BF16),
            pltpu.VMEM((8, 128), jnp.int32),
            pltpu.SMEM((8, 128), jnp.int32),
            pltpu.VMEM((shards, 128), jnp.int32),
            pltpu.SMEM((shards, 128), jnp.int32),
            pltpu.VMEM((pages * heads, head), F32),
            pltpu.VMEM((reqs, heads, head), F32),
            pltpu.VMEM((pages * heads, 128), F32),
            pltpu.VMEM((reqs, kv), F32),
            pltpu.VMEM((units, heads, head), F32),
            pltpu.VMEM((units, heads, head), F32),
            pltpu.VMEM((units, heads, head), F32),
            pltpu.VMEM((reqs, heads, head), F32),
            pltpu.VMEM((reqs, width), BF16),
            pltpu.VMEM((shards, reqs, width), BF16),
            pltpu.VMEM((tps, reqs, columns), BF16),
            pltpu.VMEM((tps, reqs, columns), BF16),
            pltpu.VMEM((rows // 2, 128), BF16),
            pltpu.VMEM((tps, rows // 2, 128), BF16),
            pltpu.VMEM((rows, panels * rank), BF16),
            pltpu.VMEM((shards, reqs, columns), BF16),
            pltpu.VMEM((shards, reqs, columns), BF16),
            dma((8,)), dma((3,)), dma((tps,)), dma((2,)),
            dma((shards,)), dma((shards,)), dma((shards,)), dma((shards,)), dma((shards,)), dma((shards,)),
            dma((tps,)), dma((tps,)), dma((tps,)), dma((tps,)),
            dma((shards,)), dma((shards,)),
        ],
        compiler_params=pltpu.CompilerParams(
            collective_id=0, has_side_effects=True, vmem_limit_bytes=62 * 1024 * 1024
        ),
    )(
        request_page_table.T,
        cached_length.reshape(1, -1),
        move_holder_shard.reshape(1, -1),
        move_page_index.reshape(1, -1),
        request_adapter.reshape(1, -1),
        adapter_storage_slot.reshape(1, -1),
        queries,
        fresh_key_value.reshape(reqs, kv),
        key_value_pool.reshape(pages, page_len, kv),
        output_projection,
        jnp.swapaxes(adapter_down_panels, 1, 2).reshape(panels * rank, width),
        adapter_up_panels.reshape(panels * rank, columns),
    )


def solution(mesh):
    shards, tps = mesh.shape["req"], mesh.shape["tp"]
    return jax.shard_map(
        functools.partial(local, shards, tps),
        mesh=mesh,
        in_specs=(
            P("req", "tp"),
            P("req", "tp", None),
            P("req", None, "tp", None),
            P("req", None),
            P("req"),
            P("req", None),
            P("req"),
            P("req"),
            P(),
            P("tp", None),
            P("req", "tp", None),
            P("req", None, "tp"),
        ),
        out_specs=P("req", "tp"),
        check_vma=False,
    )
```

```python
import functools
import math

import jax
import jax.numpy as jnp
from jax import lax
from jax.experimental import pallas as pl
from jax.experimental.pallas import tpu as pltpu
from jax.sharding import PartitionSpec as P

CAP = 4
MASKED = -1e30
F32 = jnp.float32
BF16 = jnp.bfloat16
META = 16
GROUP = 4


def iota(shape, dim):
    return lax.broadcasted_iota(jnp.int32, shape, dim)


def matmul(a, b):
    return lax.dot_general(a, b, (((1,), (0,)), ((), ())), preferred_element_type=F32)


def matmul_t(a, b):
    return lax.dot_general(a, b, (((1,), (1,)), ((), ())), preferred_element_type=F32)


def as_column(row):
    n = row.shape[1]
    return jnp.sum(jnp.where(iota((n, n), 0) == iota((n, n), 1), row, 0.0), axis=1, keepdims=True)


def as_row(column):
    n = column.shape[0]
    return jnp.sum(jnp.where(iota((n, n), 0) == iota((n, n), 1), column, 0.0), axis=0, keepdims=True)


def page_partials(queries, pages, live, head):
    heads = queries.shape[0] // len(pages)
    rows = [slice(k * heads, (k + 1) * heads) for k in range(len(pages))]
    scores = [matmul_t(queries[rows[k]].astype(BF16), page[:, :head]) for k, page in enumerate(pages)]
    scores = jnp.concatenate(scores, axis=0) * (1.0 / math.sqrt(head))
    there = iota(scores.shape, 1).astype(F32) < live
    top = jnp.max(jnp.where(there, scores, MASKED), axis=1, keepdims=True)
    weights = jnp.where(there, jnp.exp(scores - top), 0.0).astype(BF16).astype(F32)
    total = jnp.sum(weights, axis=1, keepdims=True)
    parts = [matmul(weights[rows[k]].astype(BF16), page[:, head:]) for k, page in enumerate(pages)]
    return top, total, jnp.concatenate(parts, axis=0)


def kernel(
    shards, tps,
    table_in, length_in, holder_in, index_in, adapter_in, storage_in, q_in, fresh_in, pool, w, down, up,
    out,
    table, length, holder, index, adapter, storage, q, fresh,
    pool_v, w_v, down_v, up_v, qmsg, qgot, rmsg, rgot, pick_v, pick_s, info_v, info_s,
    qown, qrh, own_live, fresh_v, o_u, m_u, l_u, att_f, att_b, att_all, psend, pgot,
    lsend, lgot, bsend, bgot,
    in_sem, load_sem, w_sem, small_sem, info_sem, q_sent, q_came, r_sent, r_came, a_sent, a_came,
    p_sent, p_came, l_sent, l_came, b_sent, b_came,
):
    me, tp = lax.axis_index("req"), lax.axis_index("tp")
    reqs, width = q.shape
    head = fresh.shape[1] // 2
    heads = width // head
    pages, page_len, _ = pool.shape
    moves = holder.shape[1]
    page_slots = table.shape[0]
    panels = storage.shape[1] // shards
    rank = down.shape[0] // panels
    columns = out.shape[1]
    qrows = CAP * heads

    barrier = pltpu.get_barrier_semaphore()

    @pl.loop(1, shards)
    def _(off):
        pl.semaphore_signal(barrier, inc=1, device_id=(lax.rem(me + off, shards), tp), device_id_type=pl.DeviceIdType.MESH)

    @pl.loop(1, tps)
    def _(off):
        pl.semaphore_signal(barrier, inc=1, device_id=(me, lax.rem(tp + off, tps)), device_id_type=pl.DeviceIdType.MESH)

    small_copies = [
        pltpu.make_async_copy(source, here, in_sem.at[n])
        for n, (source, here) in enumerate(
            (
                (holder_in, holder), (index_in, index), (table_in, table), (length_in, length),
                (q_in, q), (adapter_in, adapter), (storage_in, storage), (fresh_in, fresh),
            )
        )
    ]
    for copy in small_copies:
        copy.start()
    pool_copy = pltpu.make_async_copy(pool, pool_v, load_sem.at[0])
    pool_copy.start()
    down_copy = pltpu.make_async_copy(down, down_v, load_sem.at[1])
    up_copy = pltpu.make_async_copy(up, up_v, load_sem.at[2])
    down_copy.start()
    up_copy.start()

    def to_req(src, dst, sent, came, peer):
        return pltpu.make_async_remote_copy(
            src_ref=src, dst_ref=dst, send_sem=sent, recv_sem=came,
            device_id=(peer, tp), device_id_type=pl.DeviceIdType.MESH,
        )

    def to_tp(src, dst, sent, came, peer):
        return pltpu.make_async_remote_copy(
            src_ref=src, dst_ref=dst, send_sem=sent, recv_sem=came,
            device_id=(me, peer), device_id_type=pl.DeviceIdType.MESH,
        )

    for copy in small_copies:
        copy.wait()

    group_of = GROUP
    groups = shards // group_of
    across = group_of
    x, y = lax.rem(me, across), me // across

    def neighbours(group, way):
        found = []
        for k in range(group_of):
            dx, dy = k, lax.rem(k + group + 1, groups)
            found.append(lax.rem(y + way * dy + groups, groups) * across + lax.rem(x + way * dx + across, across))
        return found

    def before(group):
        return neighbours(group, -1)

    def after(group):
        return neighbours(group, 1)

    hold_row = holder[...].astype(F32)
    hold_col = as_column(hold_row)
    earlier = iota((moves, moves), 1) < iota((moves, moves), 0)
    rank_col = jnp.sum(jnp.where(earlier & (hold_col == hold_row), 1.0, 0.0), axis=1, keepdims=True)
    slot_col = hold_col * CAP + rank_col
    slot_row = as_row(slot_col)
    index_col = as_column(index[...].astype(F32))
    lengths = length[...].astype(F32)
    request = iota((1, reqs), 1).astype(F32)
    move_req = jnp.zeros((moves, 1), F32)
    move_live = jnp.zeros((moves, 1), F32)
    own_req = jnp.zeros((pages, 1), F32)
    own_tokens = jnp.zeros((pages, 1), F32)
    for j in range(page_slots):
        entry = table[j : j + 1, :]
        live = jnp.clip(lengths - float(j * page_len), 0.0, float(page_len))
        hit = entry == pages + iota((moves, reqs), 0)
        mine = entry == iota((pages, reqs), 0)
        move_req += jnp.sum(jnp.where(hit, request, 0.0), axis=1, keepdims=True)
        move_live += jnp.sum(jnp.where(hit, live, 0.0), axis=1, keepdims=True)
        own_req += jnp.sum(jnp.where(mine, request, 0.0), axis=1, keepdims=True)
        own_tokens += jnp.sum(jnp.where(mine, live, 0.0), axis=1, keepdims=True)
        place = jnp.sum(jnp.where(hit, slot_col, 0.0), axis=0, keepdims=True).astype(jnp.int32)
        pick_v[j : j + 1, 0:reqs] = jnp.where(entry < pages, entry, pages + place)

    stacked = jnp.concatenate([q[:, h * head : (h + 1) * head] for h in range(heads)], axis=0)
    hr = heads * reqs

    def spread(slot_of, rows, wanted):
        lane_req = lax.rem(iota((wanted.shape[0], hr), 1), reqs).astype(F32)
        choice = jnp.where(wanted == lane_req, 1.0, 0.0).astype(BF16)
        chosen = matmul(slot_of, choice)
        same_head = lax.rem(iota((rows, hr), 0), heads) == iota((rows, hr), 1) // reqs
        return matmul(jnp.where(same_head, chosen, 0.0).astype(BF16), stacked)

    slot_rows = shards * qrows
    to_slot = ((iota((slot_rows, moves), 0) // heads).astype(F32) == slot_row).astype(F32).astype(BF16)
    slot_q = spread(to_slot, slot_rows, move_req).astype(BF16)

    request_col = as_column(adapter[...].astype(F32))
    slots = storage.shape[1]
    request_slot = jnp.sum(
        jnp.where(request_col == iota((reqs, slots), 1).astype(F32), storage[...].astype(F32), 0.0), axis=1, keepdims=True
    )
    lane = iota((moves, 128), 1).astype(F32)
    asked = jnp.where(lane == rank_col, index_col, 0.0) + jnp.where(lane == rank_col + CAP, move_live, 0.0)
    by_holder = (iota((shards, moves), 0).astype(F32) == hold_row).astype(F32).astype(BF16)
    ask = matmul(by_holder, asked.astype(BF16))
    first = iota((META, 128), 0) == 0
    upper = iota((META, 128), 1) >= 64
    for d in range(shards):
        qmsg[d, 0:qrows, :] = slot_q[d * qrows : (d + 1) * qrows]
        qmsg[d, qrows : qrows + META, :] = jnp.where(
            upper, request_slot, jnp.where(first, ask[d : d + 1, :], 0.0)
        ).astype(BF16)

    pl.semaphore_wait(barrier, shards - 1 + tps - 1)

    def ask_copy(peer, slot):
        return to_req(qmsg.at[peer], qgot.at[slot], q_sent.at[peer], q_came.at[slot], peer)

    for group in range(groups):
        for k, peer in enumerate(after(group)):
            if not (group == groups - 1 and k == 0):
                ask_copy(peer, me).start()

    qgot[pl.ds(me, 1)] = qmsg[pl.ds(me, 1)]

    own_rows = pages * heads
    to_page = ((iota((own_rows, pages), 0) // heads) == iota((own_rows, pages), 1)).astype(F32).astype(BF16)
    qown[...] = spread(to_page, own_rows, own_req)
    own_live[...] = matmul(to_page, jnp.broadcast_to(own_tokens, (pages, 128)).astype(BF16))
    swap = (iota((hr, hr), 0) // heads == lax.rem(iota((hr, hr), 1), reqs)) & (
        lax.rem(iota((hr, hr), 0), heads) == iota((hr, hr), 1) // reqs
    )
    qrh[...] = matmul(swap.astype(F32).astype(BF16), stacked).reshape(reqs, heads, head)
    fresh_v[...] = fresh[...].astype(F32)
    pick_copy = pltpu.make_async_copy(pick_v, pick_s, small_sem.at[0])
    pick_copy.start()

    pool_copy.wait()
    w_copies = [
        pltpu.make_async_copy(w.at[:, pl.ds(c * columns, columns)], w_v.at[c], w_sem.at[c]) for c in range(tps)
    ]
    for copy in w_copies:
        copy.start()

    batch = 16

    @pl.loop(0, pages // batch)
    def _(group):
        rows = pl.ds(pl.multiple_of(group * batch * heads, batch * heads), batch * heads)
        units = pl.ds(group * batch, batch)
        top, total, part = page_partials(
            qown[rows, :], [pool_v.at[group * batch + k] for k in range(batch)], own_live[rows, 0:1], head
        )
        o_u[units] = part.reshape(batch, heads, head)
        m_u[units] = jnp.broadcast_to(top, part.shape).reshape(batch, heads, head)
        l_u[units] = jnp.broadcast_to(total, part.shape).reshape(batch, heads, head)

    def info_copy(group):
        return pltpu.make_async_copy(info_v.at[group], info_s.at[group], info_sem.at[group])

    def prepare(group):
        sources = before(group)
        for source in sources:

            @pl.when(source != me)
            def _():
                ask_copy(source, source).wait_recv()

        wanted = [qgot[source, qrows : qrows + META, :][0:1].astype(F32) for source in sources]
        info_v[group] = jnp.concatenate(wanted + wanted, axis=0).astype(jnp.int32)
        info_copy(group).start()

    prepare(0)

    block = iota((heads, 128), 1) // 32
    piece = lax.rem(iota((heads, 128), 1), 32) // 8

    def part_copy(peer, slot):
        return to_req(rmsg.at[peer], rgot.at[slot], r_sent.at[peer], r_came.at[slot], peer)

    @pl.loop(0, groups)
    def _(group):
        @pl.when(group + 1 < groups)
        def _():
            prepare(group + 1)

        info_copy(group).wait()
        sources = before(group)
        queries = jnp.concatenate([qgot[source, 0:qrows, :].astype(F32) for source in sources], axis=0)
        picked, live = [], []
        for k in range(group_of):
            for c in range(CAP):
                picked.append(pool_v.at[jnp.clip(info_s[group, k, c], 0, pages - 1)])
                live.append(jnp.full((heads, 1), info_s[group, k, CAP + c], jnp.int32))
        top, total, part = page_partials(queries, picked, jnp.concatenate(live, axis=0).astype(F32), head)
        bodies, tails = [], []
        for k in range(group_of):
            tops = jnp.zeros((heads, 128), F32)
            totals = jnp.zeros((heads, 128), F32)
            for c in range(CAP):
                rows = slice((k * CAP + c) * heads, (k * CAP + c + 1) * heads)
                tops = jnp.where(block == c, top[rows], tops)
                totals = jnp.where(block == c, total[rows], totals)
            high = tops.astype(BF16).astype(F32)
            rest = tops - high
            middle = rest.astype(BF16).astype(F32)
            sum_high = totals.astype(BF16).astype(F32)
            packed = jnp.where(
                piece == 0, high, jnp.where(piece == 1, middle, jnp.where(piece == 2, rest - middle, sum_high))
            )
            bodies.append(part[k * qrows : (k + 1) * qrows].astype(BF16))
            tails.append(jnp.concatenate([packed, totals - sum_high], axis=0).astype(BF16))
        for source, body, tail in zip(sources, bodies, tails):
            rmsg[source, 0:qrows, :] = body
            rmsg[source, qrows : qrows + META, :] = tail
        for source in sources:

            @pl.when(source != me)
            def _():
                part_copy(source, me).start()

    rgot[pl.ds(me, 1)] = rmsg[pl.ds(me, 1)]

    @pl.loop(0, groups)
    def _(group):
        sources = after(group)
        for source in sources:

            @pl.when(source != me)
            def _():
                part_copy(source, source).wait_recv()

        found = []
        for source in sources:
            part = rgot[source, 0:qrows, :].astype(F32)
            tail = rgot[source, qrows : qrows + META, :].astype(F32)
            packed = tail[0:heads]
            tops = packed + pltpu.roll(packed, 120, 1) + pltpu.roll(packed, 112, 1)
            totals = packed + tail[heads : 2 * heads]
            top = jnp.concatenate([tops[:, c * 32 : c * 32 + 1] for c in range(CAP)], axis=0)
            total = jnp.concatenate([totals[:, c * 32 + 24 : c * 32 + 25] for c in range(CAP)], axis=0)
            found.append((part, jnp.broadcast_to(top, part.shape), jnp.broadcast_to(total, part.shape)))
        for source, values in zip(sources, found):
            units = pl.ds(pages + source * CAP, CAP)
            for kept, value in zip((o_u, m_u, l_u), values):
                kept[units] = value.reshape(CAP, heads, head)

    pick_copy.wait()

    @pl.loop(0, reqs // group_of)
    def _(group):
        merged = []
        for k in range(group_of):
            r = group * group_of + k
            units = [jnp.clip(pick_s[j, r], 0, o_u.shape[0] - 1) for j in range(page_slots)]
            tops = [m_u[u] for u in units]
            new = fresh_v[pl.ds(r, 1), :]
            own = jnp.sum(qrh[r] * new[:, :head], axis=1, keepdims=True) * (1.0 / math.sqrt(head))
            overall = jnp.maximum(functools.reduce(jnp.maximum, tops), own)
            own_weight = jnp.exp(own - overall)
            above = own_weight * new[:, head:]
            below = own_weight
            for u, top in zip(units, tops):
                scale = jnp.exp(top - overall)
                above += scale * o_u[u]
                below += scale * l_u[u]
            merged.append((above / below)[None])
        att_f[pl.ds(group * group_of, group_of)] = jnp.concatenate(merged, axis=0)

    att_b[...] = jnp.concatenate([att_f[:, h, :] for h in range(heads)], axis=1).astype(BF16)

    def att_copy(peer, slot):
        return to_req(att_b, att_all.at[slot], a_sent.at[peer], a_came.at[slot], peer)

    att_all[pl.ds(me, 1)] = att_b[...][None]

    for copy in w_copies:
        copy.wait()

    def p_copy(peer, slot):
        return to_tp(psend.at[peer], pgot.at[slot], p_sent.at[peer], p_came.at[slot], peer)

    def project(step):
        peer = lax.rem(tp + step, tps)
        psend[peer] = matmul(att_b[...], w_v[peer]).astype(BF16)
        p_copy(peer, tp).start()

    steps = [list(range(1, tps))[group::groups] for group in range(groups)]
    for group in range(groups):
        peers = after(group)[1 if group == groups - 1 else 0 :]
        for peer in peers:
            att_copy(peer, me).start()

    for step in range(1, tps):
        project(step)
    total = matmul(att_b[...], w_v[tp])

    down_copy.wait()
    up_copy.wait()

    many = group_of * reqs
    half = many // 2
    left = iota((half, 128), 1) < 64
    panel_of = (iota((many, panels * rank), 1) // rank + me * panels).astype(F32)

    def l_copy(group, peer, slot):
        return to_tp(lsend.at[group], lgot.at[group, slot], l_sent.at[group, peer], l_came.at[group, slot], peer)

    def b_copy(peer, slot):
        return to_req(bsend.at[peer], bgot.at[slot], b_sent.at[peer], b_came.at[slot], peer)

    def stored_here(sources):
        tags = jnp.concatenate([qgot[source, qrows : qrows + META, :] for source in sources], axis=0).astype(F32)
        return panel_of == tags[:, 64:65]

    def go_down(group):
        sources = before(group)
        for source in sources:

            @pl.when(source != me)
            def _():
                att_copy(source, source).wait_recv()

        low = matmul_t(jnp.concatenate([att_all[source] for source in sources], axis=0), down_v[...])
        low = jnp.where(stored_here(sources), low, 0.0)
        low = low[:, :128] + low[:, 128:]
        low = low + pltpu.roll(low, 64, 1)
        low = jnp.where(left, low[:half], low[half:]).astype(BF16)
        lsend[group] = low
        lgot[group, pl.ds(tp, 1)] = low[None]

        @pl.loop(1, tps)
        def _(off):
            l_copy(group, lax.rem(tp + off, tps), tp).start()

    def go_up(group):
        sources = before(group)

        @pl.loop(1, tps)
        def _(off):
            source = lax.rem(tp + tps - off, tps)
            l_copy(group, source, source).wait_recv()

        whole = jnp.sum(lgot[group].astype(F32), axis=0).astype(BF16).astype(F32)
        turned = pltpu.roll(whole, 64, 1)
        both = jnp.concatenate([jnp.where(left, whole, turned), jnp.where(left, turned, whole)], axis=0)
        both = jnp.where(stored_here(sources), jnp.concatenate([both, both], axis=1), 0.0).astype(BF16)
        term = matmul(both, up_v[...]).astype(BF16)
        for k, source in enumerate(sources):
            bsend[source] = term[k * reqs : (k + 1) * reqs]
        for source in sources:

            @pl.when(source != me)
            def _():
                b_copy(source, me).start()

    @pl.loop(1, shards)
    def _(off):
        peer = lax.rem(me + off, shards)
        ask_copy(peer, me).wait_send()
        part_copy(peer, me).wait_send()

    ahead = 3
    for group in range(groups + ahead):
        if group < groups:
            go_down(group)
        if group >= ahead - 1 and group - ahead + 1 < groups:
            go_up(group - ahead + 1)

    @pl.loop(1, shards)
    def _(off):
        att_copy(lax.rem(me + off, shards), me).wait_send()

    @pl.loop(1, tps)
    def _(off):
        peer = lax.rem(tp + off, tps)
        p_copy(peer, tp).wait_send()
        for group in range(groups):
            l_copy(group, peer, tp).wait_send()

    def add_projected(off, total):
        source = lax.rem(tp + tps - off, tps)
        p_copy(source, source).wait_recv()
        return total + pgot[source].astype(F32)

    total = lax.fori_loop(1, tps, add_projected, total)

    total += bsend[me].astype(F32)
    for group in range(groups):
        others = slice(1 if group == groups - 1 else 0, group_of)
        for source in after(group)[others]:
            b_copy(source, source).wait_recv()
            total += bgot[source].astype(F32)
        if group == groups - 1:
            out[...] = total.astype(BF16)
        for peer in before(group)[others]:
            b_copy(peer, me).wait_send()


def local(
    shards, tps,
    queries, fresh_key_value, key_value_pool, request_page_table, cached_length, move_holder_shard, move_page_index,
    request_adapter, adapter_storage_slot, output_projection, adapter_down_panels, adapter_up_panels,
):
    reqs, width = queries.shape
    pages, page_len, _, kv = key_value_pool.shape
    head = kv // 2
    heads = width // head
    panels, _, rank = adapter_down_panels.shape
    columns = output_projection.shape[1] // tps
    qrows = CAP * heads
    units = pages + shards * CAP
    groups = shards // GROUP
    dma = pltpu.SemaphoreType.DMA
    small = pl.BlockSpec(memory_space=pltpu.VMEM)
    large = pl.BlockSpec(memory_space=pl.ANY)
    return pl.pallas_call(
        functools.partial(kernel, shards, tps),
        out_shape=jax.ShapeDtypeStruct((reqs, columns), BF16),
        in_specs=[large] * 12,
        out_specs=small,
        scratch_shapes=[
            pltpu.VMEM(request_page_table.shape[::-1], jnp.int32),
            pltpu.VMEM((1, reqs), jnp.int32),
            pltpu.VMEM((1, move_holder_shard.shape[0]), jnp.int32),
            pltpu.VMEM((1, move_holder_shard.shape[0]), jnp.int32),
            pltpu.VMEM((1, reqs), jnp.int32),
            pltpu.VMEM((1, adapter_storage_slot.shape[0]), jnp.int32),
            pltpu.VMEM((reqs, width), BF16),
            pltpu.VMEM((reqs, kv), BF16),
            pltpu.VMEM((pages, page_len, kv), BF16),
            pltpu.VMEM((tps, width, columns), BF16),
            pltpu.VMEM((panels * rank, width), BF16),
            pltpu.VMEM((panels * rank, columns), BF16),
            pltpu.VMEM((shards, qrows + META, head), BF16),
            pltpu.VMEM((shards, qrows + META, head), BF16),
            pltpu.VMEM((shards, qrows + META, head), BF16),
            pltpu.VMEM((shards, qrows + META, head), BF16),
            pltpu.VMEM((8, 128), jnp.int32),
            pltpu.SMEM((8, 128), jnp.int32),
            pltpu.VMEM((groups, 2 * GROUP, 128), jnp.int32),
            pltpu.SMEM((groups, 2 * GROUP, 128), jnp.int32),
            pltpu.VMEM((pages * heads, head), F32),
            pltpu.VMEM((reqs, heads, head), F32),
            pltpu.VMEM((pages * heads, 128), F32),
            pltpu.VMEM((reqs, kv), F32),
            pltpu.VMEM((units, heads, head), F32),
            pltpu.VMEM((units, heads, head), F32),
            pltpu.VMEM((units, heads, head), F32),
            pltpu.VMEM((reqs, heads, head), F32),
            pltpu.VMEM((reqs, width), BF16),
            pltpu.VMEM((shards, reqs, width), BF16),
            pltpu.VMEM((tps, reqs, columns), BF16),
            pltpu.VMEM((tps, reqs, columns), BF16),
            pltpu.VMEM((groups, GROUP * reqs // 2, 128), BF16),
            pltpu.VMEM((groups, tps, GROUP * reqs // 2, 128), BF16),
            pltpu.VMEM((shards, reqs, columns), BF16),
            pltpu.VMEM((shards, reqs, columns), BF16),
            dma((8,)), dma((3,)), dma((tps,)), dma((1,)), dma((groups,)),
            dma((shards,)), dma((shards,)), dma((shards,)), dma((shards,)), dma((shards,)), dma((shards,)),
            dma((tps,)), dma((tps,)), dma((groups, tps)), dma((groups, tps)),
            dma((shards,)), dma((shards,)),
        ],
        compiler_params=pltpu.CompilerParams(
            collective_id=0, has_side_effects=True, vmem_limit_bytes=48 * 1024 * 1024
        ),
    )(*(pltpu.with_memory_space_constraint(operand, pltpu.HBM) for operand in (
        request_page_table.T,
        cached_length.reshape(1, -1),
        move_holder_shard.reshape(1, -1),
        move_page_index.reshape(1, -1),
        request_adapter.reshape(1, -1),
        adapter_storage_slot.reshape(1, -1),
        queries,
        fresh_key_value.reshape(reqs, kv),
        key_value_pool.reshape(pages, page_len, kv),
        output_projection,
        jnp.swapaxes(adapter_down_panels, 1, 2).reshape(panels * rank, width),
        adapter_up_panels.reshape(panels * rank, columns),
    )))


def solution(mesh):
    shards, tps = mesh.shape["req"], mesh.shape["tp"]
    return jax.shard_map(
        functools.partial(local, shards, tps),
        mesh=mesh,
        in_specs=(
            P("req", "tp"),
            P("req", "tp", None),
            P("req", None, "tp", None),
            P("req", None),
            P("req"),
            P("req", None),
            P("req"),
            P("req"),
            P(),
            P("tp", None),
            P("req", "tp", None),
            P("req", None, "tp"),
        ),
        out_specs=P("req", "tp"),
        check_vma=False,
    )
```

```python
import functools
import math

import jax
import jax.numpy as jnp
from jax import lax
from jax.experimental import pallas as pl
from jax.experimental.pallas import tpu as pltpu
from jax.sharding import PartitionSpec as P

CAP = 4
MASKED = -1e30
F32 = jnp.float32
BF16 = jnp.bfloat16
META = 16
GROUP = 4


def iota(shape, dim):
    return lax.broadcasted_iota(jnp.int32, shape, dim)


def matmul(a, b):
    return lax.dot_general(a, b, (((1,), (0,)), ((), ())), preferred_element_type=F32)


def matmul_t(a, b):
    return lax.dot_general(a, b, (((1,), (1,)), ((), ())), preferred_element_type=F32)


def as_column(row):
    n = row.shape[1]
    return jnp.sum(jnp.where(iota((n, n), 0) == iota((n, n), 1), row, 0.0), axis=1, keepdims=True)


def as_row(column):
    n = column.shape[0]
    return jnp.sum(jnp.where(iota((n, n), 0) == iota((n, n), 1), column, 0.0), axis=0, keepdims=True)


def page_partials(queries, pages, live, head):
    heads = queries.shape[0] // len(pages)
    rows = [slice(k * heads, (k + 1) * heads) for k in range(len(pages))]
    scores = [matmul_t(queries[rows[k]].astype(BF16), page[:, :head]) for k, page in enumerate(pages)]
    scores = jnp.concatenate(scores, axis=0) * (1.0 / math.sqrt(head))
    there = iota(scores.shape, 1).astype(F32) < live
    top = jnp.max(jnp.where(there, scores, MASKED), axis=1, keepdims=True)
    weights = jnp.where(there, jnp.exp(scores - top), 0.0).astype(BF16).astype(F32)
    total = jnp.sum(weights, axis=1, keepdims=True)
    parts = [matmul(weights[rows[k]].astype(BF16), page[:, head:]) for k, page in enumerate(pages)]
    return top, total, jnp.concatenate(parts, axis=0)


def kernel(
    shards, tps,
    table_in, length_in, holder_in, index_in, adapter_in, storage_in, q_in, fresh_in, pool, w, down, up,
    out,
    table, length, holder, index, adapter, storage, q, fresh,
    pool_v, w_v, down_v, up_v, qmsg, qgot, rmsg, rgot, pick_v, pick_s, info_v, info_s,
    qown, qrh, own_live, fresh_v, o_u, m_u, l_u, att_f, att_b, att_all, psend, pgot,
    lsend, lgot, bsend, bgot,
    in_sem, load_sem, w_sem, small_sem, info_sem, q_sent, q_came, r_sent, r_came, a_sent, a_came,
    p_sent, p_came, l_sent, l_came, b_sent, b_came,
):
    me, tp = lax.axis_index("req"), lax.axis_index("tp")
    reqs, width = q.shape
    head = fresh.shape[1] // 2
    heads = width // head
    pages, page_len, _ = pool.shape
    moves = holder.shape[1]
    page_slots = table.shape[0]
    panels = storage.shape[1] // shards
    rank = down.shape[0] // panels
    columns = out.shape[1]
    qrows = CAP * heads

    barrier = pltpu.get_barrier_semaphore()

    @pl.loop(1, shards)
    def _(off):
        pl.semaphore_signal(barrier, inc=1, device_id=(lax.rem(me + off, shards), tp), device_id_type=pl.DeviceIdType.MESH)

    @pl.loop(1, tps)
    def _(off):
        pl.semaphore_signal(barrier, inc=1, device_id=(me, lax.rem(tp + off, tps)), device_id_type=pl.DeviceIdType.MESH)

    small_copies = [
        pltpu.make_async_copy(source, here, in_sem.at[n])
        for n, (source, here) in enumerate(
            (
                (holder_in, holder), (index_in, index), (table_in, table), (length_in, length),
                (q_in, q), (adapter_in, adapter), (storage_in, storage), (fresh_in, fresh),
            )
        )
    ]
    for copy in small_copies:
        copy.start()
    pool_copy = pltpu.make_async_copy(pool, pool_v, load_sem.at[0])
    pool_copy.start()
    down_copy = pltpu.make_async_copy(down, down_v, load_sem.at[1])
    up_copy = pltpu.make_async_copy(up, up_v, load_sem.at[2])
    down_copy.start()
    up_copy.start()

    def to_req(src, dst, sent, came, peer):
        return pltpu.make_async_remote_copy(
            src_ref=src, dst_ref=dst, send_sem=sent, recv_sem=came,
            device_id=(peer, tp), device_id_type=pl.DeviceIdType.MESH,
        )

    def to_tp(src, dst, sent, came, peer):
        return pltpu.make_async_remote_copy(
            src_ref=src, dst_ref=dst, send_sem=sent, recv_sem=came,
            device_id=(me, peer), device_id_type=pl.DeviceIdType.MESH,
        )

    for copy in small_copies:
        copy.wait()

    group_of = GROUP
    groups = shards // group_of
    across = group_of
    x, y = lax.rem(me, across), me // across

    def neighbours(group, way):
        found = []
        for k in range(group_of):
            dx, dy = k, lax.rem(k + group + 1, groups)
            found.append(lax.rem(y + way * dy + groups, groups) * across + lax.rem(x + way * dx + across, across))
        return found

    def before(group):
        return neighbours(group, -1)

    def after(group):
        return neighbours(group, 1)

    hold_row = holder[...].astype(F32)
    hold_col = as_column(hold_row)
    earlier = iota((moves, moves), 1) < iota((moves, moves), 0)
    rank_col = jnp.sum(jnp.where(earlier & (hold_col == hold_row), 1.0, 0.0), axis=1, keepdims=True)
    slot_col = hold_col * CAP + rank_col
    slot_row = as_row(slot_col)
    index_col = as_column(index[...].astype(F32))
    lengths = length[...].astype(F32)
    request = iota((1, reqs), 1).astype(F32)
    move_req = jnp.zeros((moves, 1), F32)
    move_live = jnp.zeros((moves, 1), F32)
    own_req = jnp.zeros((pages, 1), F32)
    own_tokens = jnp.zeros((pages, 1), F32)
    for j in range(page_slots):
        entry = table[j : j + 1, :]
        live = jnp.clip(lengths - float(j * page_len), 0.0, float(page_len))
        hit = entry == pages + iota((moves, reqs), 0)
        mine = entry == iota((pages, reqs), 0)
        move_req += jnp.sum(jnp.where(hit, request, 0.0), axis=1, keepdims=True)
        move_live += jnp.sum(jnp.where(hit, live, 0.0), axis=1, keepdims=True)
        own_req += jnp.sum(jnp.where(mine, request, 0.0), axis=1, keepdims=True)
        own_tokens += jnp.sum(jnp.where(mine, live, 0.0), axis=1, keepdims=True)
        place = jnp.sum(jnp.where(hit, slot_col, 0.0), axis=0, keepdims=True).astype(jnp.int32)
        pick_v[j : j + 1, 0:reqs] = jnp.where(entry < pages, entry, pages + place)

    stacked = jnp.concatenate([q[:, h * head : (h + 1) * head] for h in range(heads)], axis=0)
    hr = heads * reqs

    def spread(slot_of, rows, wanted):
        lane_req = lax.rem(iota((wanted.shape[0], hr), 1), reqs).astype(F32)
        choice = jnp.where(wanted == lane_req, 1.0, 0.0).astype(BF16)
        chosen = matmul(slot_of, choice)
        same_head = lax.rem(iota((rows, hr), 0), heads) == iota((rows, hr), 1) // reqs
        return matmul(jnp.where(same_head, chosen, 0.0).astype(BF16), stacked)

    slot_rows = shards * qrows
    to_slot = ((iota((slot_rows, moves), 0) // heads).astype(F32) == slot_row).astype(F32).astype(BF16)
    slot_q = spread(to_slot, slot_rows, move_req).astype(BF16)

    request_col = as_column(adapter[...].astype(F32))
    slots = storage.shape[1]
    request_slot = jnp.sum(
        jnp.where(request_col == iota((reqs, slots), 1).astype(F32), storage[...].astype(F32), 0.0), axis=1, keepdims=True
    )
    lane = iota((moves, 128), 1).astype(F32)
    asked = jnp.where(lane == rank_col, index_col, 0.0) + jnp.where(lane == rank_col + CAP, move_live, 0.0)
    by_holder = (iota((shards, moves), 0).astype(F32) == hold_row).astype(F32).astype(BF16)
    ask = matmul(by_holder, asked.astype(BF16))
    first = iota((META, 128), 0) == 0
    upper = iota((META, 128), 1) >= 64
    for d in range(shards):
        qmsg[d, 0:qrows, :] = slot_q[d * qrows : (d + 1) * qrows]
        qmsg[d, qrows : qrows + META, :] = jnp.where(
            upper, request_slot, jnp.where(first, ask[d : d + 1, :], 0.0)
        ).astype(BF16)

    pl.semaphore_wait(barrier, shards - 1 + tps - 1)

    def ask_copy(peer, slot):
        return to_req(qmsg.at[peer], qgot.at[slot], q_sent.at[peer], q_came.at[slot], peer)

    for group in range(groups):
        for k, peer in enumerate(after(group)):
            if not (group == groups - 1 and k == 0):
                ask_copy(peer, me).start()

    qgot[pl.ds(me, 1)] = qmsg[pl.ds(me, 1)]

    own_rows = pages * heads
    to_page = ((iota((own_rows, pages), 0) // heads) == iota((own_rows, pages), 1)).astype(F32).astype(BF16)
    qown[...] = spread(to_page, own_rows, own_req)
    own_live[...] = matmul(to_page, jnp.broadcast_to(own_tokens, (pages, 128)).astype(BF16))
    swap = (iota((hr, hr), 0) // heads == lax.rem(iota((hr, hr), 1), reqs)) & (
        lax.rem(iota((hr, hr), 0), heads) == iota((hr, hr), 1) // reqs
    )
    qrh[...] = matmul(swap.astype(F32).astype(BF16), stacked).reshape(reqs, heads, head)
    fresh_v[...] = fresh[...].astype(F32)
    pick_copy = pltpu.make_async_copy(pick_v, pick_s, small_sem.at[0])
    pick_copy.start()

    pool_copy.wait()
    w_copies = [
        pltpu.make_async_copy(w.at[:, pl.ds(c * columns, columns)], w_v.at[c], w_sem.at[c]) for c in range(tps)
    ]
    for copy in w_copies:
        copy.start()

    batch = 16

    @pl.loop(0, pages // batch)
    def _(group):
        rows = pl.ds(pl.multiple_of(group * batch * heads, batch * heads), batch * heads)
        units = pl.ds(group * batch, batch)
        top, total, part = page_partials(
            qown[rows, :], [pool_v.at[group * batch + k] for k in range(batch)], own_live[rows, 0:1], head
        )
        o_u[units] = part.reshape(batch, heads, head)
        m_u[units] = jnp.broadcast_to(top, part.shape).reshape(batch, heads, head)
        l_u[units] = jnp.broadcast_to(total, part.shape).reshape(batch, heads, head)

    def info_copy(group):
        return pltpu.make_async_copy(info_v.at[group], info_s.at[group], info_sem.at[group])

    def prepare(group):
        sources = before(group)
        for source in sources:

            @pl.when(source != me)
            def _():
                ask_copy(source, source).wait_recv()

        wanted = [qgot[source, qrows : qrows + META, :][0:1].astype(F32) for source in sources]
        info_v[group] = jnp.concatenate(wanted + wanted, axis=0).astype(jnp.int32)
        info_copy(group).start()

    prepare(0)

    block = iota((heads, 128), 1) // 32
    piece = lax.rem(iota((heads, 128), 1), 32) // 8

    def part_copy(peer, slot):
        return to_req(rmsg.at[peer], rgot.at[slot], r_sent.at[peer], r_came.at[slot], peer)

    @pl.loop(0, groups)
    def _(group):
        @pl.when(group + 1 < groups)
        def _():
            prepare(group + 1)

        info_copy(group).wait()
        sources = before(group)
        queries = jnp.concatenate([qgot[source, 0:qrows, :].astype(F32) for source in sources], axis=0)
        picked, live = [], []
        for k in range(group_of):
            for c in range(CAP):
                picked.append(pool_v.at[jnp.clip(info_s[group, k, c], 0, pages - 1)])
                live.append(jnp.full((heads, 1), info_s[group, k, CAP + c], jnp.int32))
        top, total, part = page_partials(queries, picked, jnp.concatenate(live, axis=0).astype(F32), head)
        bodies, tails = [], []
        for k in range(group_of):
            tops = jnp.zeros((heads, 128), F32)
            totals = jnp.zeros((heads, 128), F32)
            for c in range(CAP):
                rows = slice((k * CAP + c) * heads, (k * CAP + c + 1) * heads)
                tops = jnp.where(block == c, top[rows], tops)
                totals = jnp.where(block == c, total[rows], totals)
            high = tops.astype(BF16).astype(F32)
            rest = tops - high
            middle = rest.astype(BF16).astype(F32)
            sum_high = totals.astype(BF16).astype(F32)
            packed = jnp.where(
                piece == 0, high, jnp.where(piece == 1, middle, jnp.where(piece == 2, rest - middle, sum_high))
            )
            bodies.append(part[k * qrows : (k + 1) * qrows].astype(BF16))
            tails.append(jnp.concatenate([packed, totals - sum_high], axis=0).astype(BF16))
        for source, body, tail in zip(sources, bodies, tails):
            rmsg[source, 0:qrows, :] = body
            rmsg[source, qrows : qrows + META, :] = tail
        for source in sources:

            @pl.when(source != me)
            def _():
                part_copy(source, me).start()

    rgot[pl.ds(me, 1)] = rmsg[pl.ds(me, 1)]

    @pl.loop(0, groups)
    def _(group):
        sources = after(group)
        for source in sources:

            @pl.when(source != me)
            def _():
                part_copy(source, source).wait_recv()

        found = []
        for source in sources:
            part = rgot[source, 0:qrows, :].astype(F32)
            tail = rgot[source, qrows : qrows + META, :].astype(F32)
            packed = tail[0:heads]
            tops = packed + pltpu.roll(packed, 120, 1) + pltpu.roll(packed, 112, 1)
            totals = packed + tail[heads : 2 * heads]
            top = jnp.concatenate([tops[:, c * 32 : c * 32 + 1] for c in range(CAP)], axis=0)
            total = jnp.concatenate([totals[:, c * 32 + 24 : c * 32 + 25] for c in range(CAP)], axis=0)
            found.append((part, jnp.broadcast_to(top, part.shape), jnp.broadcast_to(total, part.shape)))
        for source, values in zip(sources, found):
            units = pl.ds(pages + source * CAP, CAP)
            for kept, value in zip((o_u, m_u, l_u), values):
                kept[units] = value.reshape(CAP, heads, head)

    pick_copy.wait()

    @pl.loop(0, 1)
    def _(_):
        merged = []
        for r in range(reqs):
            units = [jnp.clip(pick_s[j, r], 0, o_u.shape[0] - 1) for j in range(page_slots)]
            tops = [m_u[u] for u in units]
            new = fresh_v[pl.ds(r, 1), :]
            own = jnp.sum(qrh[r] * new[:, :head], axis=1, keepdims=True) * (1.0 / math.sqrt(head))
            overall = jnp.maximum(functools.reduce(jnp.maximum, tops), own)
            own_weight = jnp.exp(own - overall)
            above = own_weight * new[:, head:]
            below = own_weight
            for u, top in zip(units, tops):
                scale = jnp.exp(top - overall)
                above += scale * o_u[u]
                below += scale * l_u[u]
            merged.append((above / below)[None])
        att_f[...] = jnp.concatenate(merged, axis=0)

    att_b[...] = jnp.concatenate([att_f[:, h, :] for h in range(heads)], axis=1).astype(BF16)

    def att_copy(peer, slot):
        return to_req(att_b, att_all.at[slot], a_sent.at[peer], a_came.at[slot], peer)

    att_all[pl.ds(me, 1)] = att_b[...][None]

    for copy in w_copies:
        copy.wait()

    def p_copy(peer, slot):
        return to_tp(psend.at[peer], pgot.at[slot], p_sent.at[peer], p_came.at[slot], peer)

    def project(step):
        peer = lax.rem(tp + step, tps)
        psend[peer] = matmul(att_b[...], w_v[peer]).astype(BF16)
        p_copy(peer, tp).start()

    steps = [list(range(1, tps))[group::groups] for group in range(groups)]
    for group in range(groups):
        peers = after(group)[1 if group == groups - 1 else 0 :]
        for peer in peers:
            att_copy(peer, me).start()

    for step in range(1, tps):
        project(step)
    total = matmul(att_b[...], w_v[tp])

    down_copy.wait()
    up_copy.wait()

    many = group_of * reqs
    half = many // 2
    left = iota((half, 128), 1) < 64
    panel_of = (iota((many, panels * rank), 1) // rank + me * panels).astype(F32)

    def l_copy(group, peer, slot):
        return to_tp(lsend.at[group], lgot.at[group, slot], l_sent.at[group, peer], l_came.at[group, slot], peer)

    def b_copy(peer, slot):
        return to_req(bsend.at[peer], bgot.at[slot], b_sent.at[peer], b_came.at[slot], peer)

    def stored_here(sources):
        tags = jnp.concatenate([qgot[source, qrows : qrows + META, :] for source in sources], axis=0).astype(F32)
        return panel_of == tags[:, 64:65]

    def go_down(group):
        sources = before(group)
        for source in sources:

            @pl.when(source != me)
            def _():
                att_copy(source, source).wait_recv()

        low = matmul_t(jnp.concatenate([att_all[source] for source in sources], axis=0), down_v[...])
        low = jnp.where(stored_here(sources), low, 0.0)
        low = low[:, :128] + low[:, 128:]
        low = low + pltpu.roll(low, 64, 1)
        low = jnp.where(left, low[:half], low[half:]).astype(BF16)
        lsend[group] = low
        lgot[group, pl.ds(tp, 1)] = low[None]

        @pl.loop(1, tps)
        def _(off):
            l_copy(group, lax.rem(tp + off, tps), tp).start()

    def go_up(group):
        sources = before(group)

        @pl.loop(1, tps)
        def _(off):
            source = lax.rem(tp + tps - off, tps)
            l_copy(group, source, source).wait_recv()

        whole = jnp.sum(lgot[group].astype(F32), axis=0).astype(BF16).astype(F32)
        turned = pltpu.roll(whole, 64, 1)
        both = jnp.concatenate([jnp.where(left, whole, turned), jnp.where(left, turned, whole)], axis=0)
        both = jnp.where(stored_here(sources), jnp.concatenate([both, both], axis=1), 0.0).astype(BF16)
        term = matmul(both, up_v[...]).astype(BF16)
        for k, source in enumerate(sources):
            bsend[source] = term[k * reqs : (k + 1) * reqs]
        for source in sources:

            @pl.when(source != me)
            def _():
                b_copy(source, me).start()

    @pl.loop(1, shards)
    def _(off):
        peer = lax.rem(me + off, shards)
        ask_copy(peer, me).wait_send()
        part_copy(peer, me).wait_send()

    ahead = 3
    for group in range(groups + ahead):
        if group < groups:
            go_down(group)
        if group >= ahead - 1 and group - ahead + 1 < groups:
            go_up(group - ahead + 1)

    @pl.loop(1, shards)
    def _(off):
        att_copy(lax.rem(me + off, shards), me).wait_send()

    @pl.loop(1, tps)
    def _(off):
        peer = lax.rem(tp + off, tps)
        p_copy(peer, tp).wait_send()
        for group in range(groups):
            l_copy(group, peer, tp).wait_send()

    def add_projected(off, total):
        source = lax.rem(tp + tps - off, tps)
        p_copy(source, source).wait_recv()
        return total + pgot[source].astype(F32)

    total = lax.fori_loop(1, tps, add_projected, total)

    total += bsend[me].astype(F32)
    for group in range(groups):
        others = slice(1 if group == groups - 1 else 0, group_of)
        for source in after(group)[others]:
            b_copy(source, source).wait_recv()
            total += bgot[source].astype(F32)
        if group == groups - 1:
            out[...] = total.astype(BF16)
        for peer in before(group)[others]:
            b_copy(peer, me).wait_send()


def local(
    shards, tps,
    queries, fresh_key_value, key_value_pool, request_page_table, cached_length, move_holder_shard, move_page_index,
    request_adapter, adapter_storage_slot, output_projection, adapter_down_panels, adapter_up_panels,
):
    reqs, width = queries.shape
    pages, page_len, _, kv = key_value_pool.shape
    head = kv // 2
    heads = width // head
    panels, _, rank = adapter_down_panels.shape
    columns = output_projection.shape[1] // tps
    qrows = CAP * heads
    units = pages + shards * CAP
    groups = shards // GROUP
    dma = pltpu.SemaphoreType.DMA
    small = pl.BlockSpec(memory_space=pltpu.VMEM)
    large = pl.BlockSpec(memory_space=pl.ANY)
    return pl.pallas_call(
        functools.partial(kernel, shards, tps),
        out_shape=jax.ShapeDtypeStruct((reqs, columns), BF16),
        in_specs=[large] * 12,
        out_specs=small,
        scratch_shapes=[
            pltpu.VMEM(request_page_table.shape[::-1], jnp.int32),
            pltpu.VMEM((1, reqs), jnp.int32),
            pltpu.VMEM((1, move_holder_shard.shape[0]), jnp.int32),
            pltpu.VMEM((1, move_holder_shard.shape[0]), jnp.int32),
            pltpu.VMEM((1, reqs), jnp.int32),
            pltpu.VMEM((1, adapter_storage_slot.shape[0]), jnp.int32),
            pltpu.VMEM((reqs, width), BF16),
            pltpu.VMEM((reqs, kv), BF16),
            pltpu.VMEM((pages, page_len, kv), BF16),
            pltpu.VMEM((tps, width, columns), BF16),
            pltpu.VMEM((panels * rank, width), BF16),
            pltpu.VMEM((panels * rank, columns), BF16),
            pltpu.VMEM((shards, qrows + META, head), BF16),
            pltpu.VMEM((shards, qrows + META, head), BF16),
            pltpu.VMEM((shards, qrows + META, head), BF16),
            pltpu.VMEM((shards, qrows + META, head), BF16),
            pltpu.VMEM((8, 128), jnp.int32),
            pltpu.SMEM((8, 128), jnp.int32),
            pltpu.VMEM((groups, 2 * GROUP, 128), jnp.int32),
            pltpu.SMEM((groups, 2 * GROUP, 128), jnp.int32),
            pltpu.VMEM((pages * heads, head), F32),
            pltpu.VMEM((reqs, heads, head), F32),
            pltpu.VMEM((pages * heads, 128), F32),
            pltpu.VMEM((reqs, kv), F32),
            pltpu.VMEM((units, heads, head), F32),
            pltpu.VMEM((units, heads, head), F32),
            pltpu.VMEM((units, heads, head), F32),
            pltpu.VMEM((reqs, heads, head), F32),
            pltpu.VMEM((reqs, width), BF16),
            pltpu.VMEM((shards, reqs, width), BF16),
            pltpu.VMEM((tps, reqs, columns), BF16),
            pltpu.VMEM((tps, reqs, columns), BF16),
            pltpu.VMEM((groups, GROUP * reqs // 2, 128), BF16),
            pltpu.VMEM((groups, tps, GROUP * reqs // 2, 128), BF16),
            pltpu.VMEM((shards, reqs, columns), BF16),
            pltpu.VMEM((shards, reqs, columns), BF16),
            dma((8,)), dma((3,)), dma((tps,)), dma((1,)), dma((groups,)),
            dma((shards,)), dma((shards,)), dma((shards,)), dma((shards,)), dma((shards,)), dma((shards,)),
            dma((tps,)), dma((tps,)), dma((groups, tps)), dma((groups, tps)),
            dma((shards,)), dma((shards,)),
        ],
        compiler_params=pltpu.CompilerParams(
            collective_id=0, has_side_effects=True, vmem_limit_bytes=48 * 1024 * 1024
        ),
    )(*(pltpu.with_memory_space_constraint(operand, pltpu.HBM) for operand in (
        request_page_table.T,
        cached_length.reshape(1, -1),
        move_holder_shard.reshape(1, -1),
        move_page_index.reshape(1, -1),
        request_adapter.reshape(1, -1),
        adapter_storage_slot.reshape(1, -1),
        queries,
        fresh_key_value.reshape(reqs, kv),
        key_value_pool.reshape(pages, page_len, kv),
        output_projection,
        jnp.swapaxes(adapter_down_panels, 1, 2).reshape(panels * rank, width),
        adapter_up_panels.reshape(panels * rank, columns),
    )))


def solution(mesh):
    shards, tps = mesh.shape["req"], mesh.shape["tp"]
    return jax.shard_map(
        functools.partial(local, shards, tps),
        mesh=mesh,
        in_specs=(
            P("req", "tp"),
            P("req", "tp", None),
            P("req", None, "tp", None),
            P("req", None),
            P("req"),
            P("req", None),
            P("req"),
            P("req"),
            P(),
            P("tp", None),
            P("req", "tp", None),
            P("req", None, "tp"),
        ),
        out_specs=P("req", "tp"),
        check_vma=False,
    )
```

```python
import functools
import math

import jax
import jax.numpy as jnp
from jax import lax
from jax.experimental import pallas as pl
from jax.experimental.pallas import tpu as pltpu
from jax.sharding import PartitionSpec as P

CAP = 4
MASKED = -1e30
F32 = jnp.float32
BF16 = jnp.bfloat16
META = 16
GROUP = 4


def iota(shape, dim):
    return lax.broadcasted_iota(jnp.int32, shape, dim)


def matmul(a, b):
    return lax.dot_general(a, b, (((1,), (0,)), ((), ())), preferred_element_type=F32)


def matmul_t(a, b):
    return lax.dot_general(a, b, (((1,), (1,)), ((), ())), preferred_element_type=F32)


def as_column(row):
    n = row.shape[1]
    return jnp.sum(jnp.where(iota((n, n), 0) == iota((n, n), 1), row, 0.0), axis=1, keepdims=True)


def as_row(column):
    n = column.shape[0]
    return jnp.sum(jnp.where(iota((n, n), 0) == iota((n, n), 1), column, 0.0), axis=0, keepdims=True)


def page_partials(queries, pages, live, head):
    heads = queries.shape[0] // len(pages)
    rows = [slice(k * heads, (k + 1) * heads) for k in range(len(pages))]
    scores = [matmul_t(queries[rows[k]].astype(BF16), page[:, :head]) for k, page in enumerate(pages)]
    scores = jnp.concatenate(scores, axis=0) * (1.0 / math.sqrt(head))
    there = iota(scores.shape, 1).astype(F32) < live
    top = jnp.max(jnp.where(there, scores, MASKED), axis=1, keepdims=True)
    weights = jnp.where(there, jnp.exp(scores - top), 0.0).astype(BF16).astype(F32)
    total = jnp.sum(weights, axis=1, keepdims=True)
    parts = [matmul(weights[rows[k]].astype(BF16), page[:, head:]) for k, page in enumerate(pages)]
    return top, total, jnp.concatenate(parts, axis=0)


def kernel(
    shards, tps,
    table_in, length_in, holder_in, index_in, adapter_in, storage_in, q_in, fresh_in, pool, w, down, up,
    out,
    table, length, holder, index, adapter, storage, q, fresh,
    pool_v, w_v, down_v, down_t, here_v, up_v, qmsg, qgot, rmsg, rgot, pick_v, pick_s, info_v, info_s,
    qown, qrh, own_live, fresh_v, o_u, m_u, l_u, att_f, att_b, att_all, psend, pgot,
    lsend, lgot, bsend, bgot,
    in_sem, load_sem, w_sem, small_sem, info_sem, q_sent, q_came, r_sent, r_came, a_sent, a_came,
    p_sent, p_came, l_sent, l_came, b_sent, b_came,
):
    me, tp = lax.axis_index("req"), lax.axis_index("tp")
    reqs, width = q.shape
    head = fresh.shape[1] // 2
    heads = width // head
    pages, page_len, _ = pool.shape
    moves = holder.shape[1]
    page_slots = table.shape[0]
    panels = storage.shape[1] // shards
    rank = down.shape[0] // panels
    columns = out.shape[1]
    qrows = CAP * heads

    barrier = pltpu.get_barrier_semaphore()

    @pl.loop(1, shards)
    def _(off):
        pl.semaphore_signal(barrier, inc=1, device_id=(lax.rem(me + off, shards), tp), device_id_type=pl.DeviceIdType.MESH)

    @pl.loop(1, tps)
    def _(off):
        pl.semaphore_signal(barrier, inc=1, device_id=(me, lax.rem(tp + off, tps)), device_id_type=pl.DeviceIdType.MESH)

    small_copies = [
        pltpu.make_async_copy(source, here, in_sem.at[n])
        for n, (source, here) in enumerate(
            (
                (holder_in, holder), (index_in, index), (table_in, table), (length_in, length),
                (q_in, q), (adapter_in, adapter), (storage_in, storage), (fresh_in, fresh),
            )
        )
    ]
    for copy in small_copies:
        copy.start()
    pool_copy = pltpu.make_async_copy(pool, pool_v, load_sem.at[0])
    pool_copy.start()
    down_copy = pltpu.make_async_copy(down, down_v, load_sem.at[1])
    up_copy = pltpu.make_async_copy(up, up_v, load_sem.at[2])
    down_copy.start()
    up_copy.start()

    def to_req(src, dst, sent, came, peer):
        return pltpu.make_async_remote_copy(
            src_ref=src, dst_ref=dst, send_sem=sent, recv_sem=came,
            device_id=(peer, tp), device_id_type=pl.DeviceIdType.MESH,
        )

    def to_tp(src, dst, sent, came, peer):
        return pltpu.make_async_remote_copy(
            src_ref=src, dst_ref=dst, send_sem=sent, recv_sem=came,
            device_id=(me, peer), device_id_type=pl.DeviceIdType.MESH,
        )

    for copy in small_copies:
        copy.wait()

    group_of = GROUP
    groups = shards // group_of
    across = group_of
    x, y = lax.rem(me, across), me // across

    def neighbours(group, way):
        found = []
        for k in range(group_of):
            dx, dy = k, lax.rem(k + group + 1, groups)
            found.append(lax.rem(y + way * dy + groups, groups) * across + lax.rem(x + way * dx + across, across))
        return found

    def before(group):
        return neighbours(group, -1)

    def after(group):
        return neighbours(group, 1)

    hold_row = holder[...].astype(F32)
    hold_col = as_column(hold_row)
    earlier = iota((moves, moves), 1) < iota((moves, moves), 0)
    rank_col = jnp.sum(jnp.where(earlier & (hold_col == hold_row), 1.0, 0.0), axis=1, keepdims=True)
    slot_col = hold_col * CAP + rank_col
    slot_row = as_row(slot_col)
    index_col = as_column(index[...].astype(F32))
    lengths = length[...].astype(F32)
    request = iota((1, reqs), 1).astype(F32)
    move_req = jnp.zeros((moves, 1), F32)
    move_live = jnp.zeros((moves, 1), F32)
    own_req = jnp.zeros((pages, 1), F32)
    own_tokens = jnp.zeros((pages, 1), F32)
    for j in range(page_slots):
        entry = table[j : j + 1, :]
        live = jnp.clip(lengths - float(j * page_len), 0.0, float(page_len))
        hit = entry == pages + iota((moves, reqs), 0)
        mine = entry == iota((pages, reqs), 0)
        move_req += jnp.sum(jnp.where(hit, request, 0.0), axis=1, keepdims=True)
        move_live += jnp.sum(jnp.where(hit, live, 0.0), axis=1, keepdims=True)
        own_req += jnp.sum(jnp.where(mine, request, 0.0), axis=1, keepdims=True)
        own_tokens += jnp.sum(jnp.where(mine, live, 0.0), axis=1, keepdims=True)
        place = jnp.sum(jnp.where(hit, slot_col, 0.0), axis=0, keepdims=True).astype(jnp.int32)
        pick_v[j : j + 1, 0:reqs] = jnp.where(entry < pages, entry, pages + place)

    stacked = jnp.concatenate([q[:, h * head : (h + 1) * head] for h in range(heads)], axis=0)
    hr = heads * reqs

    def spread(slot_of, rows, wanted):
        lane_req = lax.rem(iota((wanted.shape[0], hr), 1), reqs).astype(F32)
        choice = jnp.where(wanted == lane_req, 1.0, 0.0).astype(BF16)
        chosen = matmul(slot_of, choice)
        same_head = lax.rem(iota((rows, hr), 0), heads) == iota((rows, hr), 1) // reqs
        return matmul(jnp.where(same_head, chosen, 0.0).astype(BF16), stacked)

    slot_rows = shards * qrows
    to_slot = ((iota((slot_rows, moves), 0) // heads).astype(F32) == slot_row).astype(F32).astype(BF16)
    slot_q = spread(to_slot, slot_rows, move_req).astype(BF16)

    request_col = as_column(adapter[...].astype(F32))
    slots = storage.shape[1]
    request_slot = jnp.sum(
        jnp.where(request_col == iota((reqs, slots), 1).astype(F32), storage[...].astype(F32), 0.0), axis=1, keepdims=True
    )
    lane = iota((moves, 128), 1).astype(F32)
    asked = jnp.where(lane == rank_col, index_col, 0.0) + jnp.where(lane == rank_col + CAP, move_live, 0.0)
    by_holder = (iota((shards, moves), 0).astype(F32) == hold_row).astype(F32).astype(BF16)
    ask = matmul(by_holder, asked.astype(BF16))
    first = iota((META, 128), 0) == 0
    upper = iota((META, 128), 1) >= 64
    for d in range(shards):
        qmsg[d, 0:qrows, :] = slot_q[d * qrows : (d + 1) * qrows]
        qmsg[d, qrows : qrows + META, :] = jnp.where(
            upper, request_slot, jnp.where(first, ask[d : d + 1, :], 0.0)
        ).astype(BF16)

    pl.semaphore_wait(barrier, shards - 1 + tps - 1)

    def ask_copy(peer, slot):
        return to_req(qmsg.at[peer], qgot.at[slot], q_sent.at[peer], q_came.at[slot], peer)

    for group in range(groups):
        for k, peer in enumerate(after(group)):
            if not (group == groups - 1 and k == 0):
                ask_copy(peer, me).start()

    qgot[pl.ds(me, 1)] = qmsg[pl.ds(me, 1)]

    own_rows = pages * heads
    to_page = ((iota((own_rows, pages), 0) // heads) == iota((own_rows, pages), 1)).astype(F32).astype(BF16)
    qown[...] = spread(to_page, own_rows, own_req)
    own_live[...] = matmul(to_page, jnp.broadcast_to(own_tokens, (pages, 128)).astype(BF16))
    swap = (iota((hr, hr), 0) // heads == lax.rem(iota((hr, hr), 1), reqs)) & (
        lax.rem(iota((hr, hr), 0), heads) == iota((hr, hr), 1) // reqs
    )
    qrh[...] = matmul(swap.astype(F32).astype(BF16), stacked).reshape(reqs, heads, head)
    fresh_v[...] = fresh[...].astype(F32)
    pick_copy = pltpu.make_async_copy(pick_v, pick_s, small_sem.at[0])
    pick_copy.start()

    pool_copy.wait()
    w_copies = [
        pltpu.make_async_copy(w.at[:, pl.ds(c * columns, columns)], w_v.at[c], w_sem.at[c]) for c in range(tps)
    ]
    for copy in w_copies:
        copy.start()

    batch = 16

    @pl.loop(0, pages // batch)
    def _(group):
        rows = pl.ds(pl.multiple_of(group * batch * heads, batch * heads), batch * heads)
        units = pl.ds(group * batch, batch)
        top, total, part = page_partials(
            qown[rows, :], [pool_v.at[group * batch + k] for k in range(batch)], own_live[rows, 0:1], head
        )
        o_u[units] = part.reshape(batch, heads, head)
        m_u[units] = jnp.broadcast_to(top, part.shape).reshape(batch, heads, head)
        l_u[units] = jnp.broadcast_to(total, part.shape).reshape(batch, heads, head)

    def info_copy(group):
        return pltpu.make_async_copy(info_v.at[group], info_s.at[group], info_sem.at[group])

    def prepare(group):
        sources = before(group)
        for source in sources:

            @pl.when(source != me)
            def _():
                ask_copy(source, source).wait_recv()

        wanted = [qgot[source, qrows : qrows + META, :][0:1].astype(F32) for source in sources]
        info_v[group] = jnp.concatenate(wanted + wanted, axis=0).astype(jnp.int32)
        info_copy(group).start()

    down_copy.wait()
    down_t[...] = down_v[...].T

    prepare(0)

    block = iota((heads, 128), 1) // 32
    piece = lax.rem(iota((heads, 128), 1), 32) // 8

    def part_copy(peer, slot):
        return to_req(rmsg.at[peer], rgot.at[slot], r_sent.at[peer], r_came.at[slot], peer)

    @pl.loop(0, groups)
    def _(group):
        @pl.when(group + 1 < groups)
        def _():
            prepare(group + 1)

        info_copy(group).wait()
        sources = before(group)
        queries = jnp.concatenate([qgot[source, 0:qrows, :].astype(F32) for source in sources], axis=0)
        picked, live = [], []
        for k in range(group_of):
            for c in range(CAP):
                picked.append(pool_v.at[jnp.clip(info_s[group, k, c], 0, pages - 1)])
                live.append(jnp.full((heads, 1), info_s[group, k, CAP + c], jnp.int32))
        top, total, part = page_partials(queries, picked, jnp.concatenate(live, axis=0).astype(F32), head)
        bodies, tails = [], []
        for k in range(group_of):
            tops = jnp.zeros((heads, 128), F32)
            totals = jnp.zeros((heads, 128), F32)
            for c in range(CAP):
                rows = slice((k * CAP + c) * heads, (k * CAP + c + 1) * heads)
                tops = jnp.where(block == c, top[rows], tops)
                totals = jnp.where(block == c, total[rows], totals)
            high = tops.astype(BF16).astype(F32)
            rest = tops - high
            middle = rest.astype(BF16).astype(F32)
            sum_high = totals.astype(BF16).astype(F32)
            packed = jnp.where(
                piece == 0, high, jnp.where(piece == 1, middle, jnp.where(piece == 2, rest - middle, sum_high))
            )
            bodies.append(part[k * qrows : (k + 1) * qrows].astype(BF16))
            tails.append(jnp.concatenate([packed, totals - sum_high], axis=0).astype(BF16))
        for source, body, tail in zip(sources, bodies, tails):
            rmsg[source, 0:qrows, :] = body
            rmsg[source, qrows : qrows + META, :] = tail
        for source in sources:

            @pl.when(source != me)
            def _():
                part_copy(source, me).start()

    rgot[pl.ds(me, 1)] = rmsg[pl.ds(me, 1)]

    @pl.loop(0, groups)
    def _(group):
        sources = after(group)
        for source in sources:

            @pl.when(source != me)
            def _():
                part_copy(source, source).wait_recv()

        found = []
        for source in sources:
            part = rgot[source, 0:qrows, :].astype(F32)
            tail = rgot[source, qrows : qrows + META, :].astype(F32)
            packed = tail[0:heads]
            tops = packed + pltpu.roll(packed, 120, 1) + pltpu.roll(packed, 112, 1)
            totals = packed + tail[heads : 2 * heads]
            top = jnp.concatenate([tops[:, c * 32 : c * 32 + 1] for c in range(CAP)], axis=0)
            total = jnp.concatenate([totals[:, c * 32 + 24 : c * 32 + 25] for c in range(CAP)], axis=0)
            found.append((part, jnp.broadcast_to(top, part.shape), jnp.broadcast_to(total, part.shape)))
        for source, values in zip(sources, found):
            units = pl.ds(pages + source * CAP, CAP)
            for kept, value in zip((o_u, m_u, l_u), values):
                kept[units] = value.reshape(CAP, heads, head)

    pick_copy.wait()

    @pl.loop(0, 1)
    def _(_):
        merged = []
        for r in range(reqs):
            units = [jnp.clip(pick_s[j, r], 0, o_u.shape[0] - 1) for j in range(page_slots)]
            tops = [m_u[u] for u in units]
            new = fresh_v[pl.ds(r, 1), :]
            own = jnp.sum(qrh[r] * new[:, :head], axis=1, keepdims=True) * (1.0 / math.sqrt(head))
            overall = jnp.maximum(functools.reduce(jnp.maximum, tops), own)
            own_weight = jnp.exp(own - overall)
            above = own_weight * new[:, head:]
            below = own_weight
            for u, top in zip(units, tops):
                scale = jnp.exp(top - overall)
                above += scale * o_u[u]
                below += scale * l_u[u]
            merged.append((above / below)[None])
        att_f[...] = jnp.concatenate(merged, axis=0)

    att_b[...] = jnp.concatenate([att_f[:, h, :] for h in range(heads)], axis=1).astype(BF16)

    def att_copy(peer, slot):
        return to_req(att_b, att_all.at[slot], a_sent.at[peer], a_came.at[slot], peer)

    att_all[pl.ds(me, 1)] = att_b[...][None]

    for copy in w_copies:
        copy.wait()

    def p_copy(peer, slot):
        return to_tp(psend.at[peer], pgot.at[slot], p_sent.at[peer], p_came.at[slot], peer)

    def project(step):
        peer = lax.rem(tp + step, tps)
        psend[peer] = matmul(att_b[...], w_v[peer]).astype(BF16)
        p_copy(peer, tp).start()

    steps = [list(range(1, tps))[group::groups] for group in range(groups)]
    for group in range(groups):
        peers = after(group)[1 if group == groups - 1 else 0 :]
        for peer in peers:
            att_copy(peer, me).start()

    for step in range(1, tps):
        project(step)
    total = matmul(att_b[...], w_v[tp])

    up_copy.wait()

    many = group_of * reqs
    half = many // 2
    left = iota((half, 128), 1) < 64
    panel_of = (iota((many, panels * rank), 1) // rank + me * panels).astype(F32)

    def l_copy(group, peer, slot):
        return to_tp(lsend.at[group], lgot.at[group, slot], l_sent.at[group, peer], l_came.at[group, slot], peer)

    def b_copy(peer, slot):
        return to_req(bsend.at[peer], bgot.at[slot], b_sent.at[peer], b_came.at[slot], peer)

    def stored_here(sources):
        tags = jnp.concatenate([qgot[source, qrows : qrows + META, :] for source in sources], axis=0).astype(F32)
        return panel_of == tags[:, 64:65]

    def go_down(group):
        sources = before(group)
        for source in sources:

            @pl.when(source != me)
            def _():
                att_copy(source, source).wait_recv()

        low = matmul(jnp.concatenate([att_all[source] for source in sources], axis=0), down_t[...]) * here_v[group]
        low = low[:, :128] + low[:, 128:]
        low = low + pltpu.roll(low, 64, 1)
        low = jnp.where(left, low[:half], low[half:]).astype(BF16)
        lsend[group] = low
        lgot[group, pl.ds(tp, 1)] = low[None]

        @pl.loop(1, tps)
        def _(off):
            l_copy(group, lax.rem(tp + off, tps), tp).start()

    def go_up(group):
        sources = before(group)

        @pl.loop(1, tps)
        def _(off):
            source = lax.rem(tp + tps - off, tps)
            l_copy(group, source, source).wait_recv()

        whole = jnp.sum(lgot[group].astype(F32), axis=0).astype(BF16).astype(F32)
        turned = pltpu.roll(whole, 64, 1)
        both = jnp.concatenate([jnp.where(left, whole, turned), jnp.where(left, turned, whole)], axis=0)
        both = (jnp.concatenate([both, both], axis=1) * here_v[group]).astype(BF16)
        term = matmul(both, up_v[...]).astype(BF16)
        for k, source in enumerate(sources):
            bsend[source] = term[k * reqs : (k + 1) * reqs]
        for source in sources:

            @pl.when(source != me)
            def _():
                b_copy(source, me).start()

    @pl.loop(1, shards)
    def _(off):
        peer = lax.rem(me + off, shards)
        ask_copy(peer, me).wait_send()
        part_copy(peer, me).wait_send()

    for group in range(groups):
        here_v[group] = stored_here(before(group)).astype(F32)
    ahead = 3
    for group in range(groups + ahead):
        if group < groups:
            go_down(group)
        if group >= ahead - 1 and group - ahead + 1 < groups:
            go_up(group - ahead + 1)

    @pl.loop(1, shards)
    def _(off):
        att_copy(lax.rem(me + off, shards), me).wait_send()

    @pl.loop(1, tps)
    def _(off):
        peer = lax.rem(tp + off, tps)
        p_copy(peer, tp).wait_send()
        for group in range(groups):
            l_copy(group, peer, tp).wait_send()

    def add_projected(off, total):
        source = lax.rem(tp + tps - off, tps)
        p_copy(source, source).wait_recv()
        return total + pgot[source].astype(F32)

    total = lax.fori_loop(1, tps, add_projected, total)

    total += bsend[me].astype(F32)
    for group in range(groups):
        others = slice(1 if group == groups - 1 else 0, group_of)
        for source in after(group)[others]:
            b_copy(source, source).wait_recv()
            total += bgot[source].astype(F32)
        if group == groups - 1:
            out[...] = total.astype(BF16)
        for peer in before(group)[others]:
            b_copy(peer, me).wait_send()


def local(
    shards, tps,
    queries, fresh_key_value, key_value_pool, request_page_table, cached_length, move_holder_shard, move_page_index,
    request_adapter, adapter_storage_slot, output_projection, adapter_down_panels, adapter_up_panels,
):
    reqs, width = queries.shape
    pages, page_len, _, kv = key_value_pool.shape
    head = kv // 2
    heads = width // head
    panels, _, rank = adapter_down_panels.shape
    columns = output_projection.shape[1] // tps
    qrows = CAP * heads
    units = pages + shards * CAP
    groups = shards // GROUP
    dma = pltpu.SemaphoreType.DMA
    small = pl.BlockSpec(memory_space=pltpu.VMEM)
    large = pl.BlockSpec(memory_space=pl.ANY)
    return pl.pallas_call(
        functools.partial(kernel, shards, tps),
        out_shape=jax.ShapeDtypeStruct((reqs, columns), BF16),
        in_specs=[large] * 12,
        out_specs=small,
        scratch_shapes=[
            pltpu.VMEM(request_page_table.shape[::-1], jnp.int32),
            pltpu.VMEM((1, reqs), jnp.int32),
            pltpu.VMEM((1, move_holder_shard.shape[0]), jnp.int32),
            pltpu.VMEM((1, move_holder_shard.shape[0]), jnp.int32),
            pltpu.VMEM((1, reqs), jnp.int32),
            pltpu.VMEM((1, adapter_storage_slot.shape[0]), jnp.int32),
            pltpu.VMEM((reqs, width), BF16),
            pltpu.VMEM((reqs, kv), BF16),
            pltpu.VMEM((pages, page_len, kv), BF16),
            pltpu.VMEM((tps, width, columns), BF16),
            pltpu.VMEM((panels * rank, width), BF16),
            pltpu.VMEM((width, panels * rank), BF16),
            pltpu.VMEM((groups, GROUP * reqs, panels * rank), F32),
            pltpu.VMEM((panels * rank, columns), BF16),
            pltpu.VMEM((shards, qrows + META, head), BF16),
            pltpu.VMEM((shards, qrows + META, head), BF16),
            pltpu.VMEM((shards, qrows + META, head), BF16),
            pltpu.VMEM((shards, qrows + META, head), BF16),
            pltpu.VMEM((8, 128), jnp.int32),
            pltpu.SMEM((8, 128), jnp.int32),
            pltpu.VMEM((groups, 2 * GROUP, 128), jnp.int32),
            pltpu.SMEM((groups, 2 * GROUP, 128), jnp.int32),
            pltpu.VMEM((pages * heads, head), F32),
            pltpu.VMEM((reqs, heads, head), F32),
            pltpu.VMEM((pages * heads, 128), F32),
            pltpu.VMEM((reqs, kv), F32),
            pltpu.VMEM((units, heads, head), F32),
            pltpu.VMEM((units, heads, head), F32),
            pltpu.VMEM((units, heads, head), F32),
            pltpu.VMEM((reqs, heads, head), F32),
            pltpu.VMEM((reqs, width), BF16),
            pltpu.VMEM((shards, reqs, width), BF16),
            pltpu.VMEM((tps, reqs, columns), BF16),
            pltpu.VMEM((tps, reqs, columns), BF16),
            pltpu.VMEM((groups, GROUP * reqs // 2, 128), BF16),
            pltpu.VMEM((groups, tps, GROUP * reqs // 2, 128), BF16),
            pltpu.VMEM((shards, reqs, columns), BF16),
            pltpu.VMEM((shards, reqs, columns), BF16),
            dma((8,)), dma((3,)), dma((tps,)), dma((1,)), dma((groups,)),
            dma((shards,)), dma((shards,)), dma((shards,)), dma((shards,)), dma((shards,)), dma((shards,)),
            dma((tps,)), dma((tps,)), dma((groups, tps)), dma((groups, tps)),
            dma((shards,)), dma((shards,)),
        ],
        compiler_params=pltpu.CompilerParams(
            collective_id=0, has_side_effects=True, vmem_limit_bytes=48 * 1024 * 1024
        ),
    )(*(pltpu.with_memory_space_constraint(operand, pltpu.HBM) for operand in (
        request_page_table.T,
        cached_length.reshape(1, -1),
        move_holder_shard.reshape(1, -1),
        move_page_index.reshape(1, -1),
        request_adapter.reshape(1, -1),
        adapter_storage_slot.reshape(1, -1),
        queries,
        fresh_key_value.reshape(reqs, kv),
        key_value_pool.reshape(pages, page_len, kv),
        output_projection,
        jnp.swapaxes(adapter_down_panels, 1, 2).reshape(panels * rank, width),
        adapter_up_panels.reshape(panels * rank, columns),
    )))


def solution(mesh):
    shards, tps = mesh.shape["req"], mesh.shape["tp"]
    return jax.shard_map(
        functools.partial(local, shards, tps),
        mesh=mesh,
        in_specs=(
            P("req", "tp"),
            P("req", "tp", None),
            P("req", None, "tp", None),
            P("req", None),
            P("req"),
            P("req", None),
            P("req"),
            P("req"),
            P(),
            P("tp", None),
            P("req", "tp", None),
            P("req", None, "tp"),
        ),
        out_specs=P("req", "tp"),
        check_vma=False,
    )
```

```python
import functools
import math

import jax
import jax.numpy as jnp
from jax import lax
from jax.experimental import pallas as pl
from jax.experimental.pallas import tpu as pltpu
from jax.sharding import PartitionSpec as P

CAP = 4
MASKED = -1e30
F32 = jnp.float32
BF16 = jnp.bfloat16
META = 16
GROUP = 4


def iota(shape, dim):
    return lax.broadcasted_iota(jnp.int32, shape, dim)


def matmul(a, b):
    return lax.dot_general(a, b, (((1,), (0,)), ((), ())), preferred_element_type=F32)


def matmul_t(a, b):
    return lax.dot_general(a, b, (((1,), (1,)), ((), ())), preferred_element_type=F32)


def as_column(row):
    n = row.shape[1]
    return jnp.sum(jnp.where(iota((n, n), 0) == iota((n, n), 1), row, 0.0), axis=1, keepdims=True)


def as_row(column):
    n = column.shape[0]
    return jnp.sum(jnp.where(iota((n, n), 0) == iota((n, n), 1), column, 0.0), axis=0, keepdims=True)


def page_partials(queries, pages, live, head):
    heads = queries.shape[0] // len(pages)
    rows = [slice(k * heads, (k + 1) * heads) for k in range(len(pages))]
    scores = [matmul_t(queries[rows[k]].astype(BF16), page[:, :head]) for k, page in enumerate(pages)]
    scores = jnp.concatenate(scores, axis=0) * (1.0 / math.sqrt(head))
    there = iota(scores.shape, 1).astype(F32) < live
    top = jnp.max(jnp.where(there, scores, MASKED), axis=1, keepdims=True)
    weights = jnp.where(there, jnp.exp(scores - top), 0.0).astype(BF16).astype(F32)
    total = jnp.sum(weights, axis=1, keepdims=True)
    parts = [matmul(weights[rows[k]].astype(BF16), page[:, head:]) for k, page in enumerate(pages)]
    return top, total, jnp.concatenate(parts, axis=0)


def kernel(
    shards, tps,
    table_in, length_in, holder_in, index_in, adapter_in, storage_in, q_in, fresh_in, pool, w, down, up,
    out,
    table, length, holder, index, adapter, storage, q, fresh,
    pool_v, w_v, down_v, up_v, qmsg, qgot, rmsg, rgot, pick_v, pick_s, info_v, info_s,
    qown, qrh, own_live, fresh_v, o_u, m_u, l_u, att_f, att_b, att_all, psend, pgot,
    lsend, lgot, bsend, bgot,
    in_sem, load_sem, w_sem, small_sem, info_sem, q_sent, q_came, r_sent, r_came, a_sent, a_came,
    p_sent, p_came, l_sent, l_came, b_sent, b_came,
):
    me, tp = lax.axis_index("req"), lax.axis_index("tp")
    reqs, width = q.shape
    head = fresh.shape[1] // 2
    heads = width // head
    pages, page_len, _ = pool.shape
    moves = holder.shape[1]
    page_slots = table.shape[0]
    panels = storage.shape[1] // shards
    rank = down.shape[0] // panels
    columns = out.shape[1]
    qrows = CAP * heads

    barrier = pltpu.get_barrier_semaphore()

    @pl.loop(1, shards)
    def _(off):
        pl.semaphore_signal(barrier, inc=1, device_id=(lax.rem(me + off, shards), tp), device_id_type=pl.DeviceIdType.MESH)

    @pl.loop(1, tps)
    def _(off):
        pl.semaphore_signal(barrier, inc=1, device_id=(me, lax.rem(tp + off, tps)), device_id_type=pl.DeviceIdType.MESH)

    small_copies = [
        pltpu.make_async_copy(source, here, in_sem.at[n])
        for n, (source, here) in enumerate(
            (
                (holder_in, holder), (index_in, index), (table_in, table), (length_in, length),
                (q_in, q), (adapter_in, adapter), (storage_in, storage), (fresh_in, fresh),
            )
        )
    ]
    for copy in small_copies:
        copy.start()
    pool_copy = pltpu.make_async_copy(pool, pool_v, load_sem.at[0])
    pool_copy.start()
    down_copy = pltpu.make_async_copy(down, down_v, load_sem.at[1])
    up_copy = pltpu.make_async_copy(up, up_v, load_sem.at[2])
    down_copy.start()
    up_copy.start()

    def to_req(src, dst, sent, came, peer):
        return pltpu.make_async_remote_copy(
            src_ref=src, dst_ref=dst, send_sem=sent, recv_sem=came,
            device_id=(peer, tp), device_id_type=pl.DeviceIdType.MESH,
        )

    def to_tp(src, dst, sent, came, peer):
        return pltpu.make_async_remote_copy(
            src_ref=src, dst_ref=dst, send_sem=sent, recv_sem=came,
            device_id=(me, peer), device_id_type=pl.DeviceIdType.MESH,
        )

    for copy in small_copies:
        copy.wait()

    group_of = GROUP
    groups = shards // group_of
    across = group_of
    x, y = lax.rem(me, across), me // across

    def neighbours(group, way):
        found = []
        for k in range(group_of):
            dx, dy = k, lax.rem(k + group + 1, groups)
            found.append(lax.rem(y + way * dy + groups, groups) * across + lax.rem(x + way * dx + across, across))
        return found

    def before(group):
        return neighbours(group, -1)

    def after(group):
        return neighbours(group, 1)

    hold_row = holder[...].astype(F32)
    hold_col = as_column(hold_row)
    earlier = iota((moves, moves), 1) < iota((moves, moves), 0)
    rank_col = jnp.sum(jnp.where(earlier & (hold_col == hold_row), 1.0, 0.0), axis=1, keepdims=True)
    slot_col = hold_col * CAP + rank_col
    slot_row = as_row(slot_col)
    index_col = as_column(index[...].astype(F32))
    lengths = length[...].astype(F32)
    request = iota((1, reqs), 1).astype(F32)
    move_req = jnp.zeros((moves, 1), F32)
    move_live = jnp.zeros((moves, 1), F32)
    own_req = jnp.zeros((pages, 1), F32)
    own_tokens = jnp.zeros((pages, 1), F32)
    for j in range(page_slots):
        entry = table[j : j + 1, :]
        live = jnp.clip(lengths - float(j * page_len), 0.0, float(page_len))
        hit = entry == pages + iota((moves, reqs), 0)
        mine = entry == iota((pages, reqs), 0)
        move_req += jnp.sum(jnp.where(hit, request, 0.0), axis=1, keepdims=True)
        move_live += jnp.sum(jnp.where(hit, live, 0.0), axis=1, keepdims=True)
        own_req += jnp.sum(jnp.where(mine, request, 0.0), axis=1, keepdims=True)
        own_tokens += jnp.sum(jnp.where(mine, live, 0.0), axis=1, keepdims=True)
        place = jnp.sum(jnp.where(hit, slot_col, 0.0), axis=0, keepdims=True).astype(jnp.int32)
        pick_v[j : j + 1, 0:reqs] = jnp.where(entry < pages, entry, pages + place)

    stacked = jnp.concatenate([q[:, h * head : (h + 1) * head] for h in range(heads)], axis=0)
    hr = heads * reqs

    def spread(slot_of, rows, wanted):
        lane_req = lax.rem(iota((wanted.shape[0], hr), 1), reqs).astype(F32)
        choice = jnp.where(wanted == lane_req, 1.0, 0.0).astype(BF16)
        chosen = matmul(slot_of, choice)
        same_head = lax.rem(iota((rows, hr), 0), heads) == iota((rows, hr), 1) // reqs
        return matmul(jnp.where(same_head, chosen, 0.0).astype(BF16), stacked)

    slot_rows = shards * qrows
    to_slot = ((iota((slot_rows, moves), 0) // heads).astype(F32) == slot_row).astype(F32).astype(BF16)
    slot_q = spread(to_slot, slot_rows, move_req).astype(BF16)

    request_col = as_column(adapter[...].astype(F32))
    slots = storage.shape[1]
    request_slot = jnp.sum(
        jnp.where(request_col == iota((reqs, slots), 1).astype(F32), storage[...].astype(F32), 0.0), axis=1, keepdims=True
    )
    lane = iota((moves, 128), 1).astype(F32)
    asked = jnp.where(lane == rank_col, index_col, 0.0) + jnp.where(lane == rank_col + CAP, move_live, 0.0)
    by_holder = (iota((shards, moves), 0).astype(F32) == hold_row).astype(F32).astype(BF16)
    ask = matmul(by_holder, asked.astype(BF16))
    first = iota((META, 128), 0) == 0
    upper = iota((META, 128), 1) >= 64
    for d in range(shards):
        qmsg[d, 0:qrows, :] = slot_q[d * qrows : (d + 1) * qrows]
        qmsg[d, qrows : qrows + META, :] = jnp.where(
            upper, request_slot, jnp.where(first, ask[d : d + 1, :], 0.0)
        ).astype(BF16)

    pl.semaphore_wait(barrier, shards - 1 + tps - 1)

    def ask_copy(peer, slot):
        return to_req(qmsg.at[peer], qgot.at[slot], q_sent.at[peer], q_came.at[slot], peer)

    for group in range(groups):
        for k, peer in enumerate(after(group)):
            if not (group == groups - 1 and k == 0):
                ask_copy(peer, me).start()

    qgot[pl.ds(me, 1)] = qmsg[pl.ds(me, 1)]

    own_rows = pages * heads
    to_page = ((iota((own_rows, pages), 0) // heads) == iota((own_rows, pages), 1)).astype(F32).astype(BF16)
    qown[...] = spread(to_page, own_rows, own_req)
    own_live[...] = matmul(to_page, jnp.broadcast_to(own_tokens, (pages, 128)).astype(BF16))
    swap = (iota((hr, hr), 0) // heads == lax.rem(iota((hr, hr), 1), reqs)) & (
        lax.rem(iota((hr, hr), 0), heads) == iota((hr, hr), 1) // reqs
    )
    qrh[...] = matmul(swap.astype(F32).astype(BF16), stacked).reshape(reqs, heads, head)
    fresh_v[...] = fresh[...].astype(F32)
    pick_copy = pltpu.make_async_copy(pick_v, pick_s, small_sem.at[0])
    pick_copy.start()

    pool_copy.wait()
    w_copies = [
        pltpu.make_async_copy(w.at[:, pl.ds(c * columns, columns)], w_v.at[c], w_sem.at[c]) for c in range(tps)
    ]
    for copy in w_copies:
        copy.start()

    batch = 16

    @pl.loop(0, pages // batch)
    def _(group):
        rows = pl.ds(pl.multiple_of(group * batch * heads, batch * heads), batch * heads)
        units = pl.ds(group * batch, batch)
        top, total, part = page_partials(
            qown[rows, :], [pool_v.at[group * batch + k] for k in range(batch)], own_live[rows, 0:1], head
        )
        o_u[units] = part.reshape(batch, heads, head)
        m_u[units] = jnp.broadcast_to(top, part.shape).reshape(batch, heads, head)
        l_u[units] = jnp.broadcast_to(total, part.shape).reshape(batch, heads, head)

    def info_copy(group):
        return pltpu.make_async_copy(info_v.at[group], info_s.at[group], info_sem.at[group])

    def prepare(group):
        sources = before(group)
        for source in sources:

            @pl.when(source != me)
            def _():
                ask_copy(source, source).wait_recv()

        wanted = [qgot[source, qrows : qrows + META, :][0:1].astype(F32) for source in sources]
        info_v[group] = jnp.concatenate(wanted + wanted, axis=0).astype(jnp.int32)
        info_copy(group).start()

    prepare(0)

    block = iota((heads, 128), 1) // 32
    piece = lax.rem(iota((heads, 128), 1), 32) // 8

    def part_copy(peer, slot):
        return to_req(rmsg.at[peer], rgot.at[slot], r_sent.at[peer], r_came.at[slot], peer)

    @pl.loop(0, groups)
    def _(group):
        @pl.when(group + 1 < groups)
        def _():
            prepare(group + 1)

        info_copy(group).wait()
        sources = before(group)
        queries = jnp.concatenate([qgot[source, 0:qrows, :].astype(F32) for source in sources], axis=0)
        picked, live = [], []
        for k in range(group_of):
            for c in range(CAP):
                picked.append(pool_v.at[jnp.clip(info_s[group, k, c], 0, pages - 1)])
                live.append(jnp.full((heads, 1), info_s[group, k, CAP + c], jnp.int32))
        top, total, part = page_partials(queries, picked, jnp.concatenate(live, axis=0).astype(F32), head)
        bodies, tails = [], []
        for k in range(group_of):
            tops = jnp.zeros((heads, 128), F32)
            totals = jnp.zeros((heads, 128), F32)
            for c in range(CAP):
                rows = slice((k * CAP + c) * heads, (k * CAP + c + 1) * heads)
                tops = jnp.where(block == c, top[rows], tops)
                totals = jnp.where(block == c, total[rows], totals)
            high = tops.astype(BF16).astype(F32)
            rest = tops - high
            middle = rest.astype(BF16).astype(F32)
            sum_high = totals.astype(BF16).astype(F32)
            packed = jnp.where(
                piece == 0, high, jnp.where(piece == 1, middle, jnp.where(piece == 2, rest - middle, sum_high))
            )
            bodies.append(part[k * qrows : (k + 1) * qrows].astype(BF16))
            tails.append(jnp.concatenate([packed, totals - sum_high], axis=0).astype(BF16))
        for source, body, tail in zip(sources, bodies, tails):
            rmsg[source, 0:qrows, :] = body
            rmsg[source, qrows : qrows + META, :] = tail
        for source in sources:

            @pl.when(source != me)
            def _():
                part_copy(source, me).start()

    rgot[pl.ds(me, 1)] = rmsg[pl.ds(me, 1)]

    @pl.loop(0, groups)
    def _(group):
        sources = after(group)
        for source in sources:

            @pl.when(source != me)
            def _():
                part_copy(source, source).wait_recv()

        found = []
        for source in sources:
            part = rgot[source, 0:qrows, :].astype(F32)
            tail = rgot[source, qrows : qrows + META, :].astype(F32)
            packed = tail[0:heads]
            tops = packed + pltpu.roll(packed, 120, 1) + pltpu.roll(packed, 112, 1)
            totals = packed + tail[heads : 2 * heads]
            top = jnp.concatenate([tops[:, c * 32 : c * 32 + 1] for c in range(CAP)], axis=0)
            total = jnp.concatenate([totals[:, c * 32 + 24 : c * 32 + 25] for c in range(CAP)], axis=0)
            found.append((part, jnp.broadcast_to(top, part.shape), jnp.broadcast_to(total, part.shape)))
        for source, values in zip(sources, found):
            units = pl.ds(pages + source * CAP, CAP)
            for kept, value in zip((o_u, m_u, l_u), values):
                kept[units] = value.reshape(CAP, heads, head)

    pick_copy.wait()

    @pl.loop(0, 1)
    def _(_):
        merged = []
        for r in range(reqs):
            units = [jnp.clip(pick_s[j, r], 0, o_u.shape[0] - 1) for j in range(page_slots)]
            tops = [m_u[u] for u in units]
            new = fresh_v[pl.ds(r, 1), :]
            own = jnp.sum(qrh[r] * new[:, :head], axis=1, keepdims=True) * (1.0 / math.sqrt(head))
            overall = jnp.maximum(functools.reduce(jnp.maximum, tops), own)
            own_weight = jnp.exp(own - overall)
            above = own_weight * new[:, head:]
            below = own_weight
            for u, top in zip(units, tops):
                scale = jnp.exp(top - overall)
                above += scale * o_u[u]
                below += scale * l_u[u]
            merged.append((above / below)[None])
        att_f[...] = jnp.concatenate(merged, axis=0)

    att_b[...] = jnp.concatenate([att_f[:, h, :] for h in range(heads)], axis=1).astype(BF16)

    def att_copy(peer, slot):
        return to_req(att_b, att_all.at[slot], a_sent.at[peer], a_came.at[slot], peer)

    att_all[pl.ds(me, 1)] = att_b[...][None]

    for copy in w_copies:
        copy.wait()

    def p_copy(peer, slot):
        return to_tp(psend.at[peer], pgot.at[slot], p_sent.at[peer], p_came.at[slot], peer)

    def project(step):
        peer = lax.rem(tp + step, tps)
        psend[peer] = matmul(att_b[...], w_v[peer]).astype(BF16)

    steps = [list(range(1, tps))[group::groups] for group in range(groups)]
    for group in range(groups):
        peers = after(group)[1 if group == groups - 1 else 0 :]
        for peer in peers:
            att_copy(peer, me).start()

    for step in range(1, tps):
        project(step)
    total = matmul(att_b[...], w_v[tp])

    down_copy.wait()
    up_copy.wait()

    many = group_of * reqs
    half = many // 2
    left = iota((half, 128), 1) < 64
    panel_of = (iota((many, panels * rank), 1) // rank + me * panels).astype(F32)

    def l_copy(group, peer, slot):
        return to_tp(lsend.at[group], lgot.at[group, slot], l_sent.at[group, peer], l_came.at[group, slot], peer)

    def b_copy(peer, slot):
        return to_req(bsend.at[peer], bgot.at[slot], b_sent.at[peer], b_came.at[slot], peer)

    def stored_here(sources):
        tags = jnp.concatenate([qgot[source, qrows : qrows + META, :] for source in sources], axis=0).astype(F32)
        return panel_of == tags[:, 64:65]

    def go_down(group):
        sources = before(group)
        for source in sources:

            @pl.when(source != me)
            def _():
                att_copy(source, source).wait_recv()

        low = matmul_t(jnp.concatenate([att_all[source] for source in sources], axis=0), down_v[...])
        low = jnp.where(stored_here(sources), low, 0.0)
        low = low[:, :128] + low[:, 128:]
        low = low + pltpu.roll(low, 64, 1)
        low = jnp.where(left, low[:half], low[half:]).astype(BF16)
        lsend[group] = low
        lgot[group, pl.ds(tp, 1)] = low[None]

        @pl.loop(1, tps)
        def _(off):
            l_copy(group, lax.rem(tp + off, tps), tp).start()

    def go_up(group):
        sources = before(group)

        @pl.loop(1, tps)
        def _(off):
            source = lax.rem(tp + tps - off, tps)
            l_copy(group, source, source).wait_recv()

        whole = jnp.sum(lgot[group].astype(F32), axis=0).astype(BF16).astype(F32)
        turned = pltpu.roll(whole, 64, 1)
        both = jnp.concatenate([jnp.where(left, whole, turned), jnp.where(left, turned, whole)], axis=0)
        both = jnp.where(stored_here(sources), jnp.concatenate([both, both], axis=1), 0.0).astype(BF16)
        term = matmul(both, up_v[...]).astype(BF16)
        for k, source in enumerate(sources):
            bsend[source] = term[k * reqs : (k + 1) * reqs]
        for source in sources:

            @pl.when(source != me)
            def _():
                b_copy(source, me).start()

    @pl.loop(1, shards)
    def _(off):
        peer = lax.rem(me + off, shards)
        ask_copy(peer, me).wait_send()
        part_copy(peer, me).wait_send()

    ahead = 3
    for group in range(groups + ahead):
        if group < groups:
            go_down(group)
        if group == 3:
            @pl.loop(1, tps)
            def _(off):
                p_copy(lax.rem(tp + off, tps), tp).start()

        if group >= ahead - 1 and group - ahead + 1 < groups:
            go_up(group - ahead + 1)

    @pl.loop(1, shards)
    def _(off):
        att_copy(lax.rem(me + off, shards), me).wait_send()

    @pl.loop(1, tps)
    def _(off):
        peer = lax.rem(tp + off, tps)
        p_copy(peer, tp).wait_send()
        for group in range(groups):
            l_copy(group, peer, tp).wait_send()

    def add_projected(off, total):
        source = lax.rem(tp + tps - off, tps)
        p_copy(source, source).wait_recv()
        return total + pgot[source].astype(F32)

    total = lax.fori_loop(1, tps, add_projected, total)

    total += bsend[me].astype(F32)
    for group in range(groups):
        others = slice(1 if group == groups - 1 else 0, group_of)
        for source in after(group)[others]:
            b_copy(source, source).wait_recv()
            total += bgot[source].astype(F32)
        if group == groups - 1:
            out[...] = total.astype(BF16)
        for peer in before(group)[others]:
            b_copy(peer, me).wait_send()


def local(
    shards, tps,
    queries, fresh_key_value, key_value_pool, request_page_table, cached_length, move_holder_shard, move_page_index,
    request_adapter, adapter_storage_slot, output_projection, adapter_down_panels, adapter_up_panels,
):
    reqs, width = queries.shape
    pages, page_len, _, kv = key_value_pool.shape
    head = kv // 2
    heads = width // head
    panels, _, rank = adapter_down_panels.shape
    columns = output_projection.shape[1] // tps
    qrows = CAP * heads
    units = pages + shards * CAP
    groups = shards // GROUP
    dma = pltpu.SemaphoreType.DMA
    small = pl.BlockSpec(memory_space=pltpu.VMEM)
    large = pl.BlockSpec(memory_space=pl.ANY)
    return pl.pallas_call(
        functools.partial(kernel, shards, tps),
        out_shape=jax.ShapeDtypeStruct((reqs, columns), BF16),
        in_specs=[large] * 12,
        out_specs=small,
        scratch_shapes=[
            pltpu.VMEM(request_page_table.shape[::-1], jnp.int32),
            pltpu.VMEM((1, reqs), jnp.int32),
            pltpu.VMEM((1, move_holder_shard.shape[0]), jnp.int32),
            pltpu.VMEM((1, move_holder_shard.shape[0]), jnp.int32),
            pltpu.VMEM((1, reqs), jnp.int32),
            pltpu.VMEM((1, adapter_storage_slot.shape[0]), jnp.int32),
            pltpu.VMEM((reqs, width), BF16),
            pltpu.VMEM((reqs, kv), BF16),
            pltpu.VMEM((pages, page_len, kv), BF16),
            pltpu.VMEM((tps, width, columns), BF16),
            pltpu.VMEM((panels * rank, width), BF16),
            pltpu.VMEM((panels * rank, columns), BF16),
            pltpu.VMEM((shards, qrows + META, head), BF16),
            pltpu.VMEM((shards, qrows + META, head), BF16),
            pltpu.VMEM((shards, qrows + META, head), BF16),
            pltpu.VMEM((shards, qrows + META, head), BF16),
            pltpu.VMEM((8, 128), jnp.int32),
            pltpu.SMEM((8, 128), jnp.int32),
            pltpu.VMEM((groups, 2 * GROUP, 128), jnp.int32),
            pltpu.SMEM((groups, 2 * GROUP, 128), jnp.int32),
            pltpu.VMEM((pages * heads, head), F32),
            pltpu.VMEM((reqs, heads, head), F32),
            pltpu.VMEM((pages * heads, 128), F32),
            pltpu.VMEM((reqs, kv), F32),
            pltpu.VMEM((units, heads, head), F32),
            pltpu.VMEM((units, heads, head), F32),
            pltpu.VMEM((units, heads, head), F32),
            pltpu.VMEM((reqs, heads, head), F32),
            pltpu.VMEM((reqs, width), BF16),
            pltpu.VMEM((shards, reqs, width), BF16),
            pltpu.VMEM((tps, reqs, columns), BF16),
            pltpu.VMEM((tps, reqs, columns), BF16),
            pltpu.VMEM((groups, GROUP * reqs // 2, 128), BF16),
            pltpu.VMEM((groups, tps, GROUP * reqs // 2, 128), BF16),
            pltpu.VMEM((shards, reqs, columns), BF16),
            pltpu.VMEM((shards, reqs, columns), BF16),
            dma((8,)), dma((3,)), dma((tps,)), dma((1,)), dma((groups,)),
            dma((shards,)), dma((shards,)), dma((shards,)), dma((shards,)), dma((shards,)), dma((shards,)),
            dma((tps,)), dma((tps,)), dma((groups, tps)), dma((groups, tps)),
            dma((shards,)), dma((shards,)),
        ],
        compiler_params=pltpu.CompilerParams(
            collective_id=0, has_side_effects=True, vmem_limit_bytes=48 * 1024 * 1024
        ),
    )(*(pltpu.with_memory_space_constraint(operand, pltpu.HBM) for operand in (
        request_page_table.T,
        cached_length.reshape(1, -1),
        move_holder_shard.reshape(1, -1),
        move_page_index.reshape(1, -1),
        request_adapter.reshape(1, -1),
        adapter_storage_slot.reshape(1, -1),
        queries,
        fresh_key_value.reshape(reqs, kv),
        key_value_pool.reshape(pages, page_len, kv),
        output_projection,
        jnp.swapaxes(adapter_down_panels, 1, 2).reshape(panels * rank, width),
        adapter_up_panels.reshape(panels * rank, columns),
    )))


def solution(mesh):
    shards, tps = mesh.shape["req"], mesh.shape["tp"]
    return jax.shard_map(
        functools.partial(local, shards, tps),
        mesh=mesh,
        in_specs=(
            P("req", "tp"),
            P("req", "tp", None),
            P("req", None, "tp", None),
            P("req", None),
            P("req"),
            P("req", None),
            P("req"),
            P("req"),
            P(),
            P("tp", None),
            P("req", "tp", None),
            P("req", None, "tp"),
        ),
        out_specs=P("req", "tp"),
        check_vma=False,
    )
```
